256 devices in a mesh: expert: 32 (over y, z), dp: 8 (over x, core).
Axes of the slice: x: 4, y: 4, z: 8, core: 2. Of those that a mesh axis runs over, the one named last changes fastest.
Arguments:
- tokens: bfloat16 [32768, 1024], P(('expert', 'dp')), may hold values from -6 to 6
- out_grad: bfloat16 [32768, 1024], P(('expert', 'dp')), may hold values from -6 to 6
- expert_ids: int32 [32768, 8], P(('expert', 'dp')), may hold values from 0 to 127, all different within a row; in each aligned block of 128 rows (0 to 127, 128 to 255, ...) at most 10 rows name the same one
- gate_weights: bfloat16 [32768, 8], P(('expert', 'dp')), may hold values from 0.019897461 to 0.3984375
- keep_flags: int32 [32768], P(('expert', 'dp')), may hold values 0 or 1
- gate_proj: bfloat16 [256, 512, 640], P(('expert', 'dp')), may hold values from -0.1875 to 0.1875
- up_proj: bfloat16 [256, 512, 640], P(('expert', 'dp')), may hold values from -0.1875 to 0.1875
- down_proj: bfloat16 [256, 640, 512], P(('expert', 'dp')), may hold values from -0.25 to 0.25
Outputs:
- grad_tokens: bfloat16 [32768, 1024], P(('expert', 'dp'))
- grad_gates: bfloat16 [32768, 8], P(('expert', 'dp'))
- grad_gate_proj: bfloat16 [256, 512, 640], P(('expert', 'dp'))
- grad_up_proj: bfloat16 [256, 512, 640], P(('expert', 'dp'))
- grad_down_proj: bfloat16 [256, 640, 512], P(('expert', 'dp'))
The draws below stay inside these ranges and needn't reach their ends.
Inputs may be any that keep to these rules, and one draw needn't show every extreme that they name: `expert_ids`: each token names 8 different experts; the 128 rows of one device name no expert more than 10 times, a bound that some block reaches.
All inputs are finite; a program needn't handle non-finite values. No bound on the sum of `keep_flags` on one device may be relied on, other than what follows from the above.
Results may differ from the reference program's by a relative error of at most 0.012.
Values may be sent and summed in bfloat16 or wider, within the bound.
A program may use at most 128 MiB of HBM per device.

```python
import math
import jax
import jax.numpy as jnp
import numpy as np
from jax import lax

D = 1024
FFE = 640
TOP = 8
TOK_DEV = 128
EXPERTS = 128
CAP = 10
TOKENS = 32768
SLABS = 256
N_EXPERT = 32
N_DP = 8


def place_ends(values, stream_key, smallest, high):
    index_at = [jax.random.randint(jax.random.fold_in(stream_key, axis), (), 0, length) for axis, length in enumerate(values.shape)]
    widest = values.shape.index(max(values.shape))
    neighbour = index_at[:widest] + [(index_at[widest] + 1) % values.shape[widest]] + index_at[widest + 1:]
    return values.at[tuple(index_at)].set(smallest).at[tuple(neighbour)].set(high)


def block_scale(stream_key, shape, cuts, least, largest):
    loudness = 1.0
    for dim, shards_of in cuts:
        steps = jax.random.uniform(jax.random.fold_in(jax.random.fold_in(stream_key, 6), dim), (shards_of,), jnp.float32, least / len(cuts), largest / len(cuts))
        loudness = loudness * jnp.repeat(jnp.exp(steps), shape[dim] // shards_of).reshape((-1,) + (1,) * (len(shape) - 1 - dim))
    return loudness


def assign_block(own_key, own, number, rows, amount, top, most, lean):
    order = jax.random.permutation(own_key, amount)
    packed, usual = load_shares(amount, rows * top, most, lean, True), load_shares(amount, rows * top, most, lean, False)
    places = jnp.arange(amount)

    def named(sizes, rotation):
        used = int((sizes > 0).sum())
        fixed = max(1, used // 4)
        moved = fixed + (places - fixed + rotation * (used - fixed)) % max(1, amount - fixed)
        return jnp.zeros((amount,), jnp.int32).at[order[jnp.where(places < fixed, places, moved)]].set(jnp.asarray(sizes, jnp.int32))

    sizes = jnp.where(number % 4 == 0, named(packed, number // 4), named(usual, number - number // 4 - 1))
    mixed = jax.random.permutation(jax.random.fold_in(own, 3), amount)
    giver, receiver = mixed[0:amount // 2 * 2:2], mixed[1:amount // 2 * 2:2]
    room = jnp.minimum(sizes[giver] - 1, most - sizes[receiver]) // 2
    room = jnp.where((giver == order[0]) | (receiver == order[0]) | (sizes[receiver] == 0), 0, jnp.maximum(room, 0))
    moved = jax.random.randint(jax.random.fold_in(own, 4), (amount // 2,), 0, 1 << 20) % (room + 1)
    sizes = sizes.at[giver].add(-moved).at[receiver].add(moved)
    labels = jnp.searchsorted(jnp.cumsum(sizes), jnp.arange(rows * top), side="right").astype(jnp.int32)
    grid = labels.reshape(top, rows).T
    grid = grid[jax.random.permutation(jax.random.fold_in(own, 1), rows)]
    rotation = jax.random.randint(jax.random.fold_in(own, 2), (rows, 1), 0, top)
    return jnp.take_along_axis(grid, (jnp.arange(top)[None, :] + rotation) % top, axis=1)


def load_shares(number_of, total, bound, lean, full):
    weights = [(1 << 20) // math.isqrt(rank ** lean) + 1 for rank in range(1, number_of + 1)]
    largest = bound if full else min(bound, max(-(-total // number_of), total * weights[0] // sum(weights)))
    least = 1 if total - largest >= number_of - 1 else 0
    given, spare = [largest] + [least] * (number_of - 1), total - largest - least * (number_of - 1)
    while spare > 0:
        free = [i for i in range(1, number_of) if given[i] < largest] or [i for i in range(1, number_of) if given[i] < bound]
        mass, remaining = sum([weights[i] for i in free]), spare
        for i in free:
            extra = min(bound - given[i], max(1, remaining * weights[i] // mass), spare)
            given[i] = given[i] + extra
            spare = spare - extra
    return np.array(given)


def noise(rng, shape, scale, reach, shards=(), kind=jnp.bfloat16):
    result = jax.random.normal(rng, shape, jnp.float32) * scale
    if len(shards) > 0:
        result = block_scale(rng, shape, shards, -0.22, 0.18) * result
    return jnp.clip(result, min=-reach, max=reach).astype(kind)


def setup_inputs(seed: int = 0) -> dict:
    arg_keys = jax.random.split(jax.random.key(seed), 9)
    tokens = noise(arg_keys[0], (TOKENS, D), 1.0, 6.0, ((0, 256),))
    out_grad = noise(arg_keys[1], (TOKENS, D), 1.0, 6.0, ((0, 256),))
    expert_ids_keys = jax.random.split(jax.random.fold_in(arg_keys[2], 1), TOKENS // TOK_DEV)
    expert_ids_turns = jax.random.permutation(jax.random.fold_in(arg_keys[2], 3), TOKENS // TOK_DEV)
    expert_ids = jax.vmap(lambda own, number: assign_block(jax.random.fold_in(arg_keys[2], 2), own, number, TOK_DEV, EXPERTS, TOP, CAP, 2))(expert_ids_keys, expert_ids_turns).reshape((TOKENS, TOP))
    gate_weights = jnp.clip(jnp.exp(math.log(0.3984375) - 2.9969585 * jax.random.uniform(arg_keys[3], (TOKENS, TOP), jnp.float32) ** block_scale(arg_keys[3], (TOKENS, TOP), ((0, 256),), -0.2, 0.2)), 0.019897461, 0.3984375).astype(jnp.bfloat16)
    keep_flags = place_ends((jax.random.randint(arg_keys[4], (TOKENS,), 0, 4) < 3).astype(jnp.int32), jax.random.fold_in(arg_keys[4], 1), 0, 1)
    gate_proj = noise(arg_keys[5], (SLABS, D // 2, FFE), D ** -0.5, 0.1875, ((0, 256),))
    up_proj = noise(arg_keys[6], (SLABS, D // 2, FFE), D ** -0.5, 0.1875, ((0, 256),))
    down_proj = noise(arg_keys[7], (SLABS, FFE, D // 2), FFE ** -0.5, 0.25, ((0, 256),))
    return dict(tokens=tokens, out_grad=out_grad, expert_ids=expert_ids, gate_weights=gate_weights, keep_flags=keep_flags, gate_proj=gate_proj, up_proj=up_proj, down_proj=down_proj)


def expert_terms(rows_x, rows_dy, route_scale, keep_rows, gate_full, up_full, down_full):
    gate_pre = jnp.dot(rows_x, gate_full, preferred_element_type=jnp.float32)
    up_pre = jnp.dot(rows_x, up_full, preferred_element_type=jnp.float32)
    gate_sig = jax.nn.sigmoid(gate_pre)
    activated = gate_pre * gate_sig * up_pre
    hidden = activated.astype(jnp.bfloat16)
    weighted = (route_scale[:, None] * activated).astype(jnp.bfloat16)
    back_hidden = jnp.dot(rows_dy, down_full.T, preferred_element_type=jnp.float32)
    outputs = jnp.dot(hidden, down_full, preferred_element_type=jnp.float32)
    gate_grad = (keep_rows * jnp.sum(outputs * rows_dy.astype(jnp.float32), axis=1)).astype(jnp.bfloat16)
    hidden_grad = route_scale[:, None] * back_hidden
    grad_gate_pre = (hidden_grad * up_pre * gate_sig * (1.0 + gate_pre * (1.0 - gate_sig))).astype(jnp.bfloat16)
    grad_up_pre = (hidden_grad * gate_pre * gate_sig).astype(jnp.bfloat16)
    row_grad = (jnp.dot(grad_gate_pre, gate_full.T, preferred_element_type=jnp.float32)
                + jnp.dot(grad_up_pre, up_full.T, preferred_element_type=jnp.float32)).astype(jnp.bfloat16)
    grad_gate = jnp.dot(rows_x.T, grad_gate_pre, preferred_element_type=jnp.float32)
    grad_up = jnp.dot(rows_x.T, grad_up_pre, preferred_element_type=jnp.float32)
    grad_down = jnp.dot(weighted.T, rows_dy, preferred_element_type=jnp.float32)
    return row_grad, gate_grad, grad_gate, grad_up, grad_down


def reference(tokens, out_grad, expert_ids, gate_weights, keep_flags, gate_proj, up_proj, down_proj):
    most_rows = N_EXPERT * N_DP * CAP
    flat_ids = expert_ids.reshape(-1).astype(jnp.int32)
    sorted_order = jnp.argsort(flat_ids, stable=True).astype(jnp.int32)
    counts = jnp.bincount(flat_ids, length=EXPERTS).astype(jnp.int32)
    starts = (jnp.cumsum(counts) - counts).astype(jnp.int32)
    padded = jnp.concatenate([sorted_order, jnp.zeros((most_rows,), jnp.int32)])
    keep_float = keep_flags.astype(jnp.float32)
    scale_flat = (gate_weights.astype(jnp.float32) * keep_float[:, None]).reshape(-1)
    gate_all = gate_proj.reshape(EXPERTS, D, FFE)
    up_all = up_proj.reshape(EXPERTS, D, FFE)
    down_all = down_proj.reshape(EXPERTS, 2, FFE, D // 2).transpose(0, 2, 1, 3).reshape(EXPERTS, FFE, D)
    positions = jnp.arange(most_rows, dtype=jnp.int32)

    def visit_expert(state_pair, expert):
        grad_rows, grad_route = state_pair
        picked = lax.dynamic_slice(padded, (starts[expert],), (most_rows,))
        live_slot = positions < counts[expert]
        owner_row = (picked // TOP).astype(jnp.int32)
        route_scale = jnp.where(live_slot, scale_flat[picked], 0.0)
        keep_rows = jnp.where(live_slot, keep_float[owner_row], 0.0)
        row_grad, gate_grad, grad_gate, grad_up, grad_down = expert_terms(
            tokens[owner_row], out_grad[owner_row], route_scale, keep_rows,
            gate_all[expert], up_all[expert], down_all[expert])
        grad_rows = grad_rows.at[owner_row].add(jnp.where(live_slot[:, None], row_grad.astype(jnp.float32), 0.0))
        grad_route = grad_route.at[picked].add(jnp.where(live_slot, gate_grad.astype(jnp.float32), 0.0))
        return (grad_rows, grad_route), (grad_gate.astype(jnp.bfloat16), grad_up.astype(jnp.bfloat16), grad_down.astype(jnp.bfloat16))

    initial = (jnp.zeros((TOKENS, D), jnp.float32), jnp.zeros((TOKENS * TOP,), jnp.float32))
    (grad_rows, grad_route), (grad_gate, grad_up, grad_down) = lax.scan(
        visit_expert, initial, jnp.arange(EXPERTS, dtype=jnp.int32))
    grad_tokens = grad_rows.astype(jnp.bfloat16)
    grad_gates = grad_route.reshape(TOKENS, TOP).astype(jnp.bfloat16)
    grad_gate_proj = grad_gate.reshape(2 * EXPERTS, D // 2, FFE)
    grad_up_proj = grad_up.reshape(2 * EXPERTS, D // 2, FFE)
    grad_down_proj = grad_down.reshape(EXPERTS, FFE, 2, D // 2).transpose(0, 2, 1, 3).reshape(2 * EXPERTS, FFE, D // 2)
    return grad_tokens, grad_gates, grad_gate_proj, grad_up_proj, grad_down_proj
```

```python
import functools

import jax
import jax.numpy as jnp
from jax import lax
from jax.experimental import pallas as pl
from jax.experimental.pallas import tpu as pltpu
from jax.sharding import PartitionSpec as P

MESH = pl.DeviceIdType.MESH
BF = jnp.bfloat16
F32 = jnp.float32

TOK = 128
NZ = 8
NX = 4
CAP = 10
MSG = NZ * CAP
PLANE = NX * NX
SLOTS = PLANE * MSG
GRP = NX * MSG
NN = (((1,), (0,)), ((), ()))
NT = (((1,), (1,)), ((), ()))
TN = (((0,), (0,)), ((), ()))


def mm(a, b, dims):
    return lax.dot_general(a, b, dims, preferred_element_type=F32)


def kernel(
    x_hbm, dy_hbm, gm_hbm, ids_ref, wg_hbm, wu_hbm, wd_hbm,
    gtok_ref, ggate_ref, ogg_hbm, ogu_hbm, ogd_hbm,
    ag, agg, pt, gt, oh, ohg, send, recv, wgu, wd, gu, q, hid, dgu,
    ds0, ds1, ret0, ret1, rs0, rr0, rs1, rr1, wsg, wsd, wrg, wrd, wog, wod, gown,
    in_sem, gm_sem, w_sem, wout_sem,
    ags, agr, agg_s, agg_r, ps, pr, bs, br, rss, rsr, ws, wr, vs, vr,
):
    e = lax.axis_index("expert")
    d = lax.axis_index("dp")
    y, z = e // NZ, e % NZ
    x, core = d // 2, d % 2
    other = 1 - core

    def dev(dx, dy, dz):
        return (((y + dy + NX) % NX) * NZ + (z + dz + NZ) % NZ, ((x + dx + NX) % NX) * 2 + core)

    mate = (e, x * 2 + other)
    half = ag.shape[2]
    chunks = ag.shape[0]
    hcol = half // 2
    hidn = hid.shape[1]

    gcp = pltpu.make_async_copy(gm_hbm, agg.at[0:TOK], gm_sem)
    gcp.start()
    incp = []
    for c in range(chunks):
        src = x_hbm if c < 2 else dy_hbm
        cp = pltpu.make_async_copy(src.at[:, pl.ds((c % 2) * half, half)], ag.at[c, 0:TOK], in_sem.at[c])
        cp.start()
        incp.append(cp)
    wl = [
        pltpu.make_async_copy(wg_hbm.at[0], wgu.at[core, :, 0:hidn], w_sem.at[0]),
        pltpu.make_async_copy(wu_hbm.at[0], wgu.at[core, :, hidn:2 * hidn], w_sem.at[1]),
        pltpu.make_async_copy(wd_hbm.at[0], wd.at[core], w_sem.at[2]),
    ]
    for cp in wl:
        cp.start()

    bar = pltpu.get_barrier_semaphore()
    for dz in (1, -1):
        pl.semaphore_signal(bar, inc=1, device_id=dev(0, 0, dz), device_id_type=MESH)
    pl.semaphore_signal(bar, inc=1, device_id=mate, device_id_type=MESH)
    for j in range(1, PLANE):
        pl.semaphore_signal(bar, inc=1, device_id=dev(j % NX, j // NX, 0), device_id_type=MESH)
    pl.semaphore_wait(bar, PLANE - 1 + 3)

    def remote(src, dst, s, r, to):
        return pltpu.make_async_remote_copy(
            src_ref=src, dst_ref=dst, send_sem=s, recv_sem=r, device_id=to, device_id_type=MESH
        )

    def block(k):
        return pl.ds(k * TOK, TOK)

    def gather_copies(c, s):
        if c < 0:
            up = remote(agg.at[block(s - 1)], agg.at[block(s)], agg_s.at[0, s - 1], agg_r.at[0, s - 1], dev(0, 0, 1))
            if s == 4:
                return [up]
            a, b = (9 - s) % NZ, 8 - s
            return [up, remote(agg.at[block(a)], agg.at[block(b)], agg_s.at[1, s - 1], agg_r.at[1, s - 1], dev(0, 0, -1))]
        a, b = (9 - s) % NZ, 8 - s
        lo = pl.ds(0, hcol) if s == 4 else pl.ds(0, half)
        hi = pl.ds(hcol, hcol) if s == 4 else pl.ds(0, half)
        return [
            remote(ag.at[c, block(s - 1), lo], ag.at[c, block(s), lo], ags.at[c, 0, s - 1], agr.at[c, 0, s - 1], dev(0, 0, 1)),
            remote(ag.at[c, block(a), hi], ag.at[c, block(b), hi], ags.at[c, 1, s - 1], agr.at[c, 1, s - 1], dev(0, 0, -1)),
        ]

    def ag_start(c, s):
        for cp in gather_copies(c, s):
            cp.start()

    def ag_step(c, s):
        for cp in gather_copies(c, s):
            cp.wait_recv()
        if s < 4:
            ag_start(c, s + 1)

    gcp.wait()
    ag_start(-1, 1)
    incp[0].wait()
    ag_start(0, 1)
    wswap = [
        remote(wg_hbm.at[0], wgu.at[core, :, 0:hidn], ws.at[0], wr.at[0], mate),
        remote(wu_hbm.at[0], wgu.at[core, :, hidn:2 * hidn], ws.at[1], wr.at[1], mate),
        remote(wd_hbm.at[0], wd.at[core], ws.at[2], wr.at[2], mate),
    ]
    wrecv = [
        remote(wg_hbm.at[0], wgu.at[other, :, 0:hidn], ws.at[0], wr.at[0], mate),
        remote(wu_hbm.at[0], wgu.at[other, :, hidn:2 * hidn], ws.at[1], wr.at[1], mate),
        remote(wd_hbm.at[0], wd.at[other], ws.at[2], wr.at[2], mate),
    ]
    for cp in wswap:
        cp.start()

    for s in range(1, 4):
        ag_step(-1, s)
        ag_step(0, s)
    incp[1].wait()
    ag_start(1, 1)
    ag_step(-1, 4)

    gall = agg[...]
    gown[...] = gall[0:TOK]
    routed = jnp.where(gall != 0, 1.0, 0.0).astype(BF)
    row = lax.broadcasted_iota(jnp.int32, (TOK, TOK), 0)
    col = lax.broadcasted_iota(jnp.int32, (TOK, TOK), 1)
    wanted = ((y + row // NX) % NX) * (NZ * NX) + z * NX + (x + row % NX) % NX
    pick = jnp.where((row < PLANE) & (col == wanted), 1.0, 0.0).astype(BF)
    earlier = jnp.where(row < col, 1.0, 0.0).astype(BF)
    rt = mm(pick, routed, NT)
    gt[...] = mm(pick, gall, NT)
    for r in range(NZ):
        mine = rt[:, r * TOK:(r + 1) * TOK]
        place = mm(mine.astype(BF), earlier, NN)
        pt[:, r * TOK:(r + 1) * TOK] = jnp.where(mine > 0.5, place, -1.0)

    prow = lax.broadcasted_iota(jnp.int32, (MSG, NZ * TOK), 0)
    pcol = lax.broadcasted_iota(jnp.int32, (MSG, NZ * TOK), 1)
    pattern = jnp.where(prow // CAP == pcol // TOK, prow % CAP, -2).astype(F32)

    def build(j, carry):
        rows = pl.ds(pl.multiple_of(j * MSG, MSG), MSG)
        hit = pattern == pt[pl.ds(j, 1), :]
        oh[rows, :] = jnp.where(hit, 1.0, 0.0).astype(BF)
        ohg[rows, :] = jnp.where(hit, gt[pl.ds(j, 1), :], 0.0).astype(BF)
        return carry

    lax.fori_loop(0, PLANE, build, 0)
    ag_step(0, 4)

    def rows_of(g):
        return pl.ds(pl.multiple_of(g * GRP, GRP), GRP)

    def exchange(src, dst, s, r, g, sign):
        for dx in range(NX):
            rows = pl.ds(pl.multiple_of(g * GRP + dx * MSG, MSG), MSG)
            cp = remote(src.at[rows], dst.at[rows], s.at[g], r.at[g], dev(sign * dx, sign * g, 0))
            if dx == 0:
                @pl.when(g > 0)
                def _():
                    cp.start()

                @pl.when(g == 0)
                def _():
                    pltpu.make_async_copy(src.at[rows], dst.at[rows], r.at[g]).start()
            else:
                cp.start()

    def arrive(dst, r, g):
        pltpu.make_async_copy(dst.at[rows_of(g)], dst.at[rows_of(g)], r.at[g]).wait()

    def sent(src, s):
        for g in range(NX):
            rows = pl.ds(MSG, GRP - MSG) if g == 0 else rows_of(g)
            pltpu.make_async_copy(src.at[rows], src.at[rows], s.at[g]).wait()

    for c in range(chunks):
        sel = oh if c < 2 else ohg
        for g in range(NX):
            res = mm(sel[g * GRP:(g + 1) * GRP, :], ag[c], NN)
            send[c, g * GRP:(g + 1) * GRP, :] = res.astype(BF)
            exchange(send.at[c], recv.at[c], ps.at[c], pr.at[c], jnp.int32(g), 1)
            if c + 1 < chunks:
                ag_step(c + 1, g + 1)
                if g == 1 and c + 2 < chunks:
                    incp[c + 2].wait()
                    ag_start(c + 2, 1)

    for cp in wl:
        cp.wait()
    for cp in wrecv:
        cp.wait_recv()
    for c in range(2):
        for g in range(NX):
            arrive(recv.at[c], pr.at[c], g)

        def first(g, carry):
            part = mm(recv[c, rows_of(g), :], wgu[c], NN)
            if c == 0:
                gu[rows_of(g), :] = part
            else:
                gu[rows_of(g), :] = gu[rows_of(g), :] + part
            return carry

        lax.fori_loop(0, NX, first, 0)

    SUB = 32

    def activation(i, carry):
        rows = pl.ds(pl.multiple_of(i * SUB, SUB), SUB)
        gpre = gu[rows, 0:hidn]
        upre = gu[rows, hidn:2 * hidn]
        sig = jax.nn.sigmoid(gpre)
        swish = gpre * sig
        hid[rows, :] = (swish * upre).astype(BF)
        gu[rows, 0:hidn] = upre * sig * (1.0 + gpre * (1.0 - sig))
        gu[rows, hidn:2 * hidn] = swish
        return carry

    lax.fori_loop(0, SLOTS // SUB, activation, 0)

    for g in range(NX):
        arrive(recv.at[2], pr.at[2], g)

    def back(g, carry):
        q[rows_of(g), :] = mm(recv[2, rows_of(g), :], wd[0], NT)
        return carry

    lax.fori_loop(0, NX, back, 0)

    expert_lane = y * (NZ * NX) + z * NX + x
    lane = lax.broadcasted_iota(jnp.int32, (SUB, TOK), 1)

    def second(g, carry):
        arrive(recv.at[3], pr.at[3], g)
        q[rows_of(g), :] = q[rows_of(g), :] + mm(recv[3, rows_of(g), :], wd[1], NT)

        def grads(i, inner):
            rows = pl.ds(pl.multiple_of(g * GRP + i * SUB, SUB), SUB)
            dh = q[rows, :]
            dgu[rows, 0:hidn] = (dh * gu[rows, 0:hidn]).astype(BF)
            dgu[rows, hidn:2 * hidn] = (dh * gu[rows, hidn:2 * hidn]).astype(BF)
            dot = jnp.sum(dh * hid[rows, :].astype(F32), axis=1, keepdims=True)
            ds0[rows, half:half + TOK] = jnp.where(lane == expert_lane, dot, 0.0).astype(BF)
            return inner

        lax.fori_loop(0, GRP // SUB, grads, 0)
        ds0[rows_of(g), 0:half] = mm(dgu[rows_of(g), :], wgu[0], NT).astype(BF)
        exchange(ds0, ret0, bs.at[0], br.at[0], g, -1)
        return carry

    lax.fori_loop(0, NX, second, 0)

    def third(g, carry):
        ds1[rows_of(g), :] = mm(dgu[rows_of(g), :], wgu[1], NT).astype(BF)
        exchange(ds1, ret1, bs.at[1], br.at[1], g, -1)
        return carry

    lax.fori_loop(0, NX, third, 0)

    MT = 256

    def other_gu(m, carry):
        cols = pl.ds(pl.multiple_of(m * MT, MT), MT)
        wsg[cols, :] = mm(recv[other, :, cols], dgu[...], TN).astype(BF)
        return carry

    lax.fori_loop(0, half // MT, other_gu, 0)
    gcopy = remote(wsg, wrg, vs.at[0], vr.at[0], mate)
    gcopy.start()
    wsd[...] = mm(hid[...], recv[2 + other], TN).astype(BF)
    dcopy = remote(wsd, wrd, vs.at[1], vr.at[1], mate)
    dcopy.start()
    gcopy.wait_recv()

    def own_gu(m, carry):
        cols = pl.ds(pl.multiple_of(m * MT, MT), MT)
        wog[cols, :] = (mm(recv[core, :, cols], dgu[...], TN) + wrg[cols, :].astype(F32)).astype(BF)
        return carry

    lax.fori_loop(0, half // MT, own_gu, 0)
    dcopy.wait_recv()
    wod[...] = (mm(hid[...], recv[2 + core], TN) + wrd[...].astype(F32)).astype(BF)
    outs = [
        pltpu.make_async_copy(wog.at[:, 0:hidn], ogg_hbm.at[0], wout_sem.at[0]),
        pltpu.make_async_copy(wog.at[:, hidn:2 * hidn], ogu_hbm.at[0], wout_sem.at[1]),
        pltpu.make_async_copy(wod, ogd_hbm.at[0], wout_sem.at[2]),
    ]
    for cp in outs:
        cp.start()

    def home(n, ret, width, cut, sbuf, rbuf, at):
        for g in range(NX):
            arrive(ret, br.at[n], g)

        def combine(m, carry):
            cols = pl.ds(pl.multiple_of(m * MT, MT), MT)
            gu[cols, at:at + width] = mm(oh[:, cols], ret[...], TN)
            return carry

        lax.fori_loop(0, NZ * TOK // MT, combine, 0)

        def part(r):
            return gu[r * TOK:(r + 1) * TOK, at:at + width]

        def hop(k, s):
            lanes = pl.ds(0, width)
            if s == 1:
                lanes = pl.ds(0, cut) if k == 0 else pl.ds(cut, width - cut)
            slot = k * 4 + s - 1
            return remote(sbuf.at[slot, :, lanes], rbuf.at[slot, :, lanes], rss.at[n, slot], rsr.at[n, slot],
                          dev(0, 0, -1 if k == 0 else 1))

        def begin(k, s):
            slot = k * 4 + s - 1
            if s == 1:
                full = part(4)
                if k == 0:
                    sbuf[slot, :, 0:cut] = full[:, 0:cut].astype(BF)
                else:
                    sbuf[slot, :, cut:width] = full[:, cut:width].astype(BF)
            else:
                r = 5 - s if k == 0 else 3 + s
                full = part(r)
                if s == 2:
                    if k == 0:
                        sbuf[slot, :, 0:cut] = (full[:, 0:cut] + rbuf[slot - 1, :, 0:cut].astype(F32)).astype(BF)
                        sbuf[slot, :, cut:width] = full[:, cut:width].astype(BF)
                    else:
                        sbuf[slot, :, 0:cut] = full[:, 0:cut].astype(BF)
                        sbuf[slot, :, cut:width] = (full[:, cut:width] + rbuf[slot - 1, :, cut:width].astype(F32)).astype(BF)
                else:
                    sbuf[slot, :, :] = (full + rbuf[slot - 1].astype(F32)).astype(BF)
            hop(k, s).start()

        for k in range(2):
            begin(k, 1)
        for s in range(2, 5):
            for k in range(2):
                hop(k, s - 1).wait_recv()
                begin(k, s)
        for k in range(2):
            hop(k, 4).wait_recv()
        for s in range(1, 5):
            for k in range(2):
                hop(k, s).wait_send()
        return part(0) + rbuf[3].astype(F32) + rbuf[7].astype(F32)

    tot0 = home(0, ret0, half + TOK, 384, rs0, rr0, 0)
    gtok_ref[:, 0:half] = tot0[:, 0:half].astype(BF)
    gate = gown[...].astype(F32)
    table = tot0[:, half:half + TOK] / jnp.where(gate != 0, gate, 1.0)
    lanes = lax.broadcasted_iota(jnp.int32, (TOK, TOK), 1)
    topn = ids_ref.shape[1]
    out = jnp.zeros((TOK, topn), F32)
    which = lax.broadcasted_iota(jnp.int32, (TOK, topn), 1)
    for j in range(topn):
        value = jnp.sum(jnp.where(lanes == ids_ref[:, j:j + 1], table, 0.0), axis=1, keepdims=True)
        out = jnp.where(which == j, value, out)
    ggate_ref[...] = out.astype(BF)

    tot1 = home(1, ret1, half, 256, rs1, rr1, half + TOK)
    gtok_ref[:, half:2 * half] = tot1.astype(BF)

    for c in range(-1, chunks):
        for s in range(1, 5):
            for cp in gather_copies(c, s):
                cp.wait_send()
    for cp in wswap:
        cp.wait_send()
    for c in range(chunks):
        sent(send.at[c], ps.at[c])
    sent(ds0, bs.at[0])
    sent(ds1, bs.at[1])
    gcopy.wait_send()
    dcopy.wait_send()
    for cp in outs:
        cp.wait()


def body(tokens, out_grad, expert_ids, gate_weights, keep_flags, gate_proj, up_proj, down_proj):
    width = tokens.shape[1]
    half = width // 2
    ff = gate_proj.shape[2]
    experts = TOK
    cols = jnp.arange(experts, dtype=jnp.int32)
    gm = jnp.sum(
        jnp.where(expert_ids[:, :, None] == cols[None, None, :], gate_weights.astype(F32)[:, :, None], 0.0), axis=1
    ).astype(BF)
    dyk = out_grad * keep_flags.astype(BF)[:, None]
    any_spec = pl.BlockSpec(memory_space=pl.ANY)
    vmem = pl.BlockSpec(memory_space=pltpu.VMEM)
    dma = pltpu.SemaphoreType.DMA
    shapes = (
        jax.ShapeDtypeStruct(tokens.shape, BF),
        jax.ShapeDtypeStruct(gate_weights.shape, BF),
        jax.ShapeDtypeStruct(gate_proj.shape, BF),
        jax.ShapeDtypeStruct(up_proj.shape, BF),
        jax.ShapeDtypeStruct(down_proj.shape, BF),
    )
    scratch = [
        pltpu.VMEM((4, NZ * TOK, half), BF),
        pltpu.VMEM((NZ * TOK, experts), BF),
        pltpu.VMEM((TOK, NZ * TOK), F32),
        pltpu.VMEM((TOK, NZ * TOK), F32),
        pltpu.VMEM((SLOTS, NZ * TOK), BF),
        pltpu.VMEM((SLOTS, NZ * TOK), BF),
        pltpu.VMEM((4, SLOTS, half), BF),
        pltpu.VMEM((4, SLOTS, half), BF),
        pltpu.VMEM((2, half, 2 * ff), BF),
        pltpu.VMEM((2, ff, half), BF),
        pltpu.VMEM((SLOTS, 2 * ff), F32),
        pltpu.VMEM((SLOTS, ff), F32),
        pltpu.VMEM((SLOTS, ff), BF),
        pltpu.VMEM((SLOTS, 2 * ff), BF),
        pltpu.VMEM((SLOTS, half + TOK), BF),
        pltpu.VMEM((SLOTS, half), BF),
        pltpu.VMEM((SLOTS, half + TOK), BF),
        pltpu.VMEM((SLOTS, half), BF),
        pltpu.VMEM((8, TOK, half + TOK), BF),
        pltpu.VMEM((8, TOK, half + TOK), BF),
        pltpu.VMEM((8, TOK, half), BF),
        pltpu.VMEM((8, TOK, half), BF),
        pltpu.VMEM((half, 2 * ff), BF),
        pltpu.VMEM((ff, half), BF),
        pltpu.VMEM((half, 2 * ff), BF),
        pltpu.VMEM((ff, half), BF),
        pltpu.VMEM((half, 2 * ff), BF),
        pltpu.VMEM((ff, half), BF),
        pltpu.VMEM((TOK, experts), BF),
        dma((4,)), dma, dma((3,)), dma((3,)),
        dma((4, 2, 4)), dma((4, 2, 4)), dma((2, 4)), dma((2, 4)),
        dma((4, NX)), dma((4, NX)), dma((2, NX)), dma((2, NX)),
        dma((2, 8)), dma((2, 8)), dma((3,)), dma((3,)), dma((2,)), dma((2,)),
    ]
    return pl.pallas_call(
        kernel,
        name="experts",
        out_shape=shapes,
        in_specs=[any_spec, any_spec, any_spec, vmem, any_spec, any_spec, any_spec],
        out_specs=(vmem, vmem, any_spec, any_spec, any_spec),
        scratch_shapes=scratch,
        compiler_params=pltpu.CompilerParams(
            collective_id=0, has_side_effects=True, vmem_limit_bytes=64 * 2**20 - 2**19
        ),
    )(tokens, dyk, gm, expert_ids, gate_proj, up_proj, down_proj)


def solution(mesh):
    both = ("expert", "dp")
    in_specs = (
        P(both, None), P(both, None), P(both, None), P(both, None), P(both),
        P(both, None, None), P(both, None, None), P(both, None, None),
    )
    out_specs = (
        P(both, None), P(both, None), P(both, None, None), P(both, None, None), P(both, None, None),
    )
    return jax.shard_map(body, mesh=mesh, in_specs=in_specs, out_specs=out_specs, check_vma=False)
```

```python
import functools

import jax
import jax.numpy as jnp
from jax import lax
from jax.experimental import pallas as pl
from jax.experimental.pallas import tpu as pltpu
from jax.sharding import PartitionSpec as P

MESH = pl.DeviceIdType.MESH
BF = jnp.bfloat16
F32 = jnp.float32

TOK = 128
NZ = 8
NX = 4
CAP = 10
MSG = NZ * CAP
PLANE = NX * NX
SLOTS = PLANE * MSG
GRP = NX * MSG
FAR = (2, 1, 3, 0)
NN = (((1,), (0,)), ((), ()))
NT = (((1,), (1,)), ((), ()))
TN = (((0,), (0,)), ((), ()))


def mm(a, b, dims):
    return lax.dot_general(a, b, dims, preferred_element_type=F32)


def kernel(
    x_hbm, dy_hbm, ids_ref, gates_ref, keep_ref, wg_hbm, wu_hbm, wd_hbm,
    gtok_hbm, ggate_ref, ogg_hbm, ogu_hbm, ogd_hbm,
    ag0, ag1, ag2, ag3, dyraw, meta, pt, gt, oh, ohg, send, inter, recv, wgu, wd, gu, q, hid, dgu,
    ds0, ds1, rint0, rint1, ret0, ret1, rsa, rra, rsb, rrb, rsc, rrc, wsg, wsd, wrg, wrd, wog, wod, gtok,
    in_sem, w_sem, wout_sem,
    ags, agr, ms, mr, xs, xr, ys, yr, bs, br, cs, cr, rss, rsr, ws, wr, vs, vr,
):
    e = lax.axis_index("expert")
    d = lax.axis_index("dp")
    y, z = e // NZ, e % NZ
    x, core = d // 2, d % 2
    other = 1 - core

    def dev(dx, dy, dz):
        return (((y + dy + NX) % NX) * NZ + (z + dz + NZ) % NZ, ((x + dx + NX) % NX) * 2 + core)

    mate = (e, x * 2 + other)
    half = ag1.shape[1]
    hidn = hid.shape[1]
    nexp = TOK
    ags_bufs = [ag0, ag1, ag2, ag3]
    quarter = half // 2
    chunks = [(0, 0, quarter), (0, quarter, quarter), (1, 0, half), (2, 0, half), (3, 0, quarter), (3, quarter, quarter)]
    starts = [0, 0, 1, 3, 5, 6]
    nchunk = len(chunks)

    incp = [
        pltpu.make_async_copy(x_hbm.at[:, 0:half], ag0.at[0:TOK], in_sem.at[0]),
        pltpu.make_async_copy(x_hbm.at[:, half:2 * half], ag1.at[0:TOK], in_sem.at[1]),
        pltpu.make_async_copy(dy_hbm, dyraw, in_sem.at[2]),
    ]
    for cp in incp:
        cp.start()
    wl = [
        pltpu.make_async_copy(wg_hbm.at[0], wgu.at[core, :, 0:hidn], w_sem.at[0]),
        pltpu.make_async_copy(wu_hbm.at[0], wgu.at[core, :, hidn:2 * hidn], w_sem.at[1]),
        pltpu.make_async_copy(wd_hbm.at[0], wd.at[core], w_sem.at[2]),
    ]

    bar = pltpu.get_barrier_semaphore()
    for dz in range(1, NZ):
        pl.semaphore_signal(bar, inc=1, device_id=dev(0, 0, dz), device_id_type=MESH)
    pl.semaphore_signal(bar, inc=1, device_id=mate, device_id_type=MESH)
    for j in range(1, PLANE):
        pl.semaphore_signal(bar, inc=1, device_id=dev(j % NX, j // NX, 0), device_id_type=MESH)

    topn = ids_ref.shape[0]
    meta[0] = jnp.concatenate([ids_ref[...].astype(F32), gates_ref[...].astype(F32)], axis=0).astype(BF)
    pl.semaphore_wait(bar, PLANE - 1 + NZ)

    def remote(src, dst, s, r, to):
        return pltpu.make_async_remote_copy(
            src_ref=src, dst_ref=dst, send_sem=s, recv_sem=r, device_id=to, device_id_type=MESH
        )

    def block(k):
        return pl.ds(k * TOK, TOK)

    def gather_copies(c, s):
        buf, lane0, lanes = chunks[c]
        ag = ags_bufs[buf]
        a, b = (9 - s) % NZ, 8 - s
        lo = hi = pl.ds(lane0, lanes)
        if s == 4:
            if lanes > nexp:
                lo, hi = pl.ds(lane0, lanes // 2), pl.ds(lane0 + lanes // 2, lanes // 2)
        ways = [
            (ag.at[block(s - 1), lo], ag.at[block(s), lo], ags.at[c, 0, s - 1], agr.at[c, 0, s - 1], dev(0, 0, 1)),
            (ag.at[block(a), hi], ag.at[block(b), hi], ags.at[c, 1, s - 1], agr.at[c, 1, s - 1], dev(0, 0, -1)),
        ]
        return [remote(*way) for way in (ways[c:c + 1] if s == 4 and lanes == nexp else ways)]

    def ag_start(c):
        for cp in gather_copies(c, 1):
            cp.start()

    def ag_step(c, s):
        for cp in gather_copies(c, s):
            cp.wait_recv()
        if s < 4:
            for cp in gather_copies(c, s + 1):
                cp.start()

    tell = [remote(meta.at[0], meta.at[k], ms.at[k], mr.at[k], dev(0, 0, k)) for k in range(1, NZ)]
    for cp in tell:
        cp.start()
    incp[0].wait()
    for c in range(nchunk):
        if starts[c] == 0:
            ag_start(c)
    wswap = [
        remote(wg_hbm.at[0], wgu.at[core, :, 0:hidn], ws.at[0], wr.at[0], mate),
        remote(wu_hbm.at[0], wgu.at[core, :, hidn:2 * hidn], ws.at[1], wr.at[1], mate),
        remote(wd_hbm.at[0], wd.at[core], ws.at[2], wr.at[2], mate),
    ]
    wrecv = [
        remote(wg_hbm.at[0], wgu.at[other, :, 0:hidn], ws.at[0], wr.at[0], mate),
        remote(wu_hbm.at[0], wgu.at[other, :, hidn:2 * hidn], ws.at[1], wr.at[1], mate),
        remote(wd_hbm.at[0], wd.at[other], ws.at[2], wr.at[2], mate),
    ]

    row = lax.broadcasted_iota(jnp.int32, (TOK, TOK), 0)
    col = lax.broadcasted_iota(jnp.int32, (TOK, TOK), 1)
    row16 = lax.broadcasted_iota(jnp.int32, (PLANE, TOK), 0)
    wanted = (((y + row16 // NX) % NX) * (NZ * NX) + z * NX + (x + row16 % NX) % NX).astype(F32)
    earlier = jnp.where(row < col, 1.0, 0.0).astype(BF)

    def route(r):
        told = meta[r].astype(F32)
        mine = jnp.zeros((PLANE, TOK), F32)
        weight = mine
        for j in range(topn):
            hit = wanted == told[j:j + 1, :]
            mine = jnp.where(hit, 1.0, mine)
            weight = jnp.where(hit, told[topn + j:topn + j + 1, :], weight)
        gt[:, r * TOK:(r + 1) * TOK] = weight
        place = mm(mine.astype(BF), earlier, NN)
        pt[:, r * TOK:(r + 1) * TOK] = jnp.where(mine > 0.5, place, -1.0)

    def mask_rows():
        incp[2].wait()
        keep = jnp.where(row == col, keep_ref[...].astype(F32), 0.0).astype(BF)
        ag2[0:TOK, :] = mm(keep, dyraw[:, 0:half], NN).astype(BF)
        ag3[0:TOK, :] = mm(keep, dyraw[:, half:2 * half], NN).astype(BF)

    prow = lax.broadcasted_iota(jnp.int32, (MSG, NZ * TOK), 0)
    pcol = lax.broadcasted_iota(jnp.int32, (MSG, NZ * TOK), 1)
    pattern = jnp.where(prow // CAP == pcol // TOK, prow % CAP, -2).astype(F32)

    def build(j, carry):
        rows = pl.ds(pl.multiple_of(j * MSG, MSG), MSG)
        oh[rows, :] = jnp.where(pattern == pt[pl.ds(j, 1), :], 1.0, 0.0).astype(BF)
        return carry

    def build_gated(j, carry):
        rows = pl.ds(pl.multiple_of(j * MSG, MSG), MSG)
        ohg[rows, :] = jnp.where(pattern == pt[pl.ds(j, 1), :], gt[pl.ds(j, 1), :], 0.0).astype(BF)
        return carry

    def rows_of(g):
        return pl.ds(pl.multiple_of(g * GRP, GRP), GRP)

    def lanes_of(c):
        return pl.ds(chunks[c][1], chunks[c][2])

    def hand_out(c, g):
        buf, at, width = chunks[c]
        sel = oh if buf < 2 else ohg
        res = mm(sel[g * GRP:(g + 1) * GRP, :], ags_bufs[buf][:, at:at + width], NN).astype(BF)
        target, base = (recv, 0) if g == 0 else (inter, (g - 1) * GRP)
        target[buf, base:base + MSG, at:at + width] = res[0:MSG]
        send[buf, g * GRP + MSG:(g + 1) * GRP, at:at + width] = res[MSG:]
        for dx in FAR[:3]:
            remote(send.at[buf, pl.ds(g * GRP + dx * MSG, MSG), lanes_of(c)],
                   target.at[buf, pl.ds(base + dx * MSG, MSG), lanes_of(c)],
                   xs.at[c, g], xr.at[c, g], dev(dx, 0, 0)).start()

    def along_y(c, g):
        buf = chunks[c][0]
        return remote(inter.at[buf, pl.ds((g - 1) * GRP, GRP), lanes_of(c)], recv.at[buf, pl.ds(g * GRP, GRP), lanes_of(c)],
                      ys.at[c, g], yr.at[c, g], dev(0, g, 0))

    def pass_on(c, g):
        came = inter.at[chunks[c][0], pl.ds((g - 1) * GRP + MSG, GRP - MSG), lanes_of(c)]
        pltpu.make_async_copy(came, came, xr.at[c, g]).wait()
        along_y(c, g).start()

    def landed(c, g):
        if g == 0:
            came = recv.at[chunks[c][0], pl.ds(MSG, GRP - MSG), lanes_of(c)]
            pltpu.make_async_copy(came, came, xr.at[c, 0]).wait()
        else:
            along_y(c, g).wait_recv()

    def tick(t, first=0, end=nchunk):
        for c in range(first, end):
            if 1 <= t - starts[c] <= 4:
                ag_step(c, t - starts[c])
        for c in range(first, end):
            if t == starts[c]:
                if c == 3:
                    mask_rows()
                ag_start(c)

    ag_step(0, 1)
    route(0)
    ag_step(1, 1)
    incp[1].wait()
    ag_start(2)
    ag_step(0, 2)
    for cp in tell:
        cp.wait_recv()
    for r in range(1, NZ):
        route(r)
    ag_step(1, 2)
    ag_step(0, 3)
    lax.fori_loop(0, PLANE, build, 0)
    ag_step(2, 1)
    ag_step(1, 3)
    ag_step(0, 4)

    def first_layer(h):
        for c in range(nchunk):
            if chunks[c][0] == h:
                for g in range(NX):
                    landed(c, g)

        def first(g, carry):
            part = mm(recv[h, rows_of(g), :], wgu[h], NN)
            if h == 0:
                gu[rows_of(g), :] = part
            else:
                gu[rows_of(g), :] = gu[rows_of(g), :] + part
            return carry

        lax.fori_loop(0, NX, first, 0)

    SUB = 32

    def activation(i, carry):
        rows = pl.ds(pl.multiple_of(i * SUB, SUB), SUB)
        gpre = gu[rows, 0:hidn]
        upre = gu[rows, hidn:2 * hidn]
        sig = jax.nn.sigmoid(gpre)
        swish = gpre * sig
        hid[rows, :] = (swish * upre).astype(BF)
        gu[rows, 0:hidn] = upre * sig * (1.0 + gpre * (1.0 - sig))
        gu[rows, hidn:2 * hidn] = swish
        return carry

    for c in range(nchunk):
        if c == 1:
            for cp in wl:
                cp.start()
            for cp in wswap:
                cp.start()
        if chunks[c][0] == 2:
            lax.fori_loop(0, PLANE, build_gated, 0)
        ahead = list(range(starts[c] + 5, starts[c + 1] + 5)) if c + 1 < nchunk else []
        for i, g in enumerate(FAR):
            hand_out(c, g)
            if c == 0 and i == 0:
                tick(3, 2)
            if c == 0 and i == 2:
                ag_step(1, 4)
                tick(4, 2)
            if c == nchunk - 2 and i == 0:
                for cp in wl:
                    cp.wait()
                for cp in wrecv:
                    cp.wait_recv()
                first_layer(0)
            if c == nchunk - 1 and i == 0:
                first_layer(1)
            if c == nchunk - 1 and i == 1:
                lax.fori_loop(0, SLOTS // SUB, activation, 0)
            if c > 0 and g > 0:
                pass_on(c - 1, g)
            if i < len(ahead) - 1:
                tick(ahead[i])
        for t in ahead[3:] if len(ahead) > 4 else ahead[-1:]:
            tick(t)

    for g in FAR[:3]:
        pass_on(nchunk - 1, g)

    for g in range(NX):
        landed(3, g)

    def back(g, carry):
        q[rows_of(g), :] = mm(recv[2, rows_of(g), :], wd[0], NT)
        return carry

    lax.fori_loop(0, NX, back, 0)

    expert_lane = y * (NZ * NX) + z * NX + x
    lane = lax.broadcasted_iota(jnp.int32, (SUB, TOK), 1)
    wide = half + nexp
    back_legs = [(ds0, rint0, ret0, 0, wide), (ds1, rint1, ret1, 0, quarter), (ds1, rint1, ret1, quarter, quarter)]

    def send_back(n, g):
        src, mid, end, lane0, lanes = back_legs[n]
        target, base = (end, 0) if g == 0 else (mid, (g - 1) * GRP)
        for dx in FAR[:3]:
            remote(src.at[pl.ds(g * GRP + dx * MSG, MSG), pl.ds(lane0, lanes)],
                   target.at[pl.ds(base + dx * MSG, MSG), pl.ds(lane0, lanes)],
                   bs.at[n, g], br.at[n, g], dev(-dx, 0, 0)).start()

    def back_along_y(n, g):
        _, mid, end, lane0, lanes = back_legs[n]
        return remote(mid.at[pl.ds((g - 1) * GRP, GRP), pl.ds(lane0, lanes)],
                      end.at[pl.ds(g * GRP, GRP), pl.ds(lane0, lanes)], cs.at[n, g], cr.at[n, g], dev(0, -g, 0))

    def pass_back(n, g):
        _, mid, _, lane0, lanes = back_legs[n]
        came = mid.at[pl.ds((g - 1) * GRP + MSG, GRP - MSG), pl.ds(lane0, lanes)]
        pltpu.make_async_copy(came, came, br.at[n, g]).wait()
        back_along_y(n, g).start()

    def returned(n, g):
        _, _, end, lane0, lanes = back_legs[n]
        if g == 0:
            came = end.at[pl.ds(MSG, GRP - MSG), pl.ds(lane0, lanes)]
            pltpu.make_async_copy(came, came, br.at[n, 0]).wait()
        else:
            back_along_y(n, g).wait_recv()

    def keep_or_send(src, mid, end, g, lanes, value):
        target, base = (end, 0) if g == 0 else (mid, (g - 1) * GRP)
        target[base:base + MSG, lanes] = value[0:MSG]
        src[g * GRP + MSG:(g + 1) * GRP, lanes] = value[MSG:]

    def second(g):
        landed(4, g)
        landed(5, g)
        group = slice(g * GRP, (g + 1) * GRP)
        q[group, :] = q[group, :] + mm(recv[3, group, :], wd[1], NT)

        def grads(k, inner):
            rows = pl.ds(pl.multiple_of(g * GRP + k * SUB, SUB), SUB)
            dh = q[rows, :]
            dgu[rows, 0:hidn] = (dh * gu[rows, 0:hidn]).astype(BF)
            dgu[rows, hidn:2 * hidn] = (dh * gu[rows, hidn:2 * hidn]).astype(BF)
            dot = jnp.sum(dh * hid[rows, :].astype(F32), axis=1, keepdims=True)
            ds0[rows, half:wide] = jnp.where(lane == expert_lane, dot, 0.0).astype(BF)
            return inner

        lax.fori_loop(0, GRP // SUB, grads, 0)
        keep_or_send(ds0, rint0, ret0, g, slice(0, half), mm(dgu[group, :], wgu[0], NT).astype(BF))
        target, base = (ret0, 0) if g == 0 else (rint0, (g - 1) * GRP)
        target[base:base + MSG, half:wide] = ds0[g * GRP:g * GRP + MSG, half:wide]
        send_back(0, g)

    def third(g):
        group = slice(g * GRP, (g + 1) * GRP)
        keep_or_send(ds1, rint1, ret1, g, slice(0, half), mm(dgu[group, :], wgu[1], NT).astype(BF))
        send_back(1, g)

    for g in (0, 2, 1, 3):
        second(g)
    for g in FAR:
        third(g)
    for g in FAR:
        send_back(2, g)
    pass_back(0, 2)

    MT = 256

    def other_gu(m, carry):
        cols = pl.ds(pl.multiple_of(m * MT, MT), MT)
        wsg[cols, :] = mm(recv[other, :, cols], dgu[...], TN).astype(BF)
        return carry

    lax.fori_loop(0, half // MT, other_gu, 0)
    gcopy = remote(wsg, wrg, vs.at[0], vr.at[0], mate)
    gcopy.start()
    pass_back(0, 1)
    wsd[...] = mm(hid[...], recv[2 + other], TN).astype(BF)
    dcopy = remote(wsd, wrd, vs.at[1], vr.at[1], mate)
    dcopy.start()

    outs = [
        pltpu.make_async_copy(wog.at[:, 0:hidn], ogg_hbm.at[0], wout_sem.at[0]),
        pltpu.make_async_copy(wog.at[:, hidn:2 * hidn], ogu_hbm.at[0], wout_sem.at[1]),
        pltpu.make_async_copy(wod, ogd_hbm.at[0], wout_sem.at[2]),
    ]

    def own_gu(m, carry):
        cols = pl.ds(pl.multiple_of(m * MT, MT), MT)
        wog[cols, :] = (mm(recv[core, :, cols], dgu[...], TN) + wrg[cols, :].astype(F32)).astype(BF)
        return carry

    def own_grads():
        gcopy.wait_recv()
        lax.fori_loop(0, half // MT, own_gu, 0)
        outs[0].start()
        outs[1].start()
        dcopy.wait_recv()
        wod[...] = (mm(hid[...], recv[2 + core], TN) + wrd[...].astype(F32)).astype(BF)
        outs[2].start()

    legs = [
        (ret0, 0, wide, 3 * nexp, rsa, rra, 0),
        (ret1, 0, quarter, nexp, rsb, rrb, wide),
        (ret1, quarter, quarter, nexp, rsc, rrc, wide + quarter),
    ]

    def part(n, r):
        width, at = legs[n][2], legs[n][6]
        return gu[r * TOK:(r + 1) * TOK, at:at + width]

    def hop(n, k, s):
        _, _, width, cut, sbuf, rbuf, _ = legs[n]
        lanes = pl.ds(0, width)
        if s == 1:
            lanes = pl.ds(0, cut) if k == 0 else pl.ds(cut, width - cut)
        slot = k * 4 + s - 1
        return remote(sbuf.at[slot, :, lanes], rbuf.at[slot, :, lanes], rss.at[n, slot], rsr.at[n, slot],
                      dev(0, 0, -1 if k == 0 else 1))

    def begin(n, k, s):
        _, _, width, cut, sbuf, rbuf, _ = legs[n]
        slot = k * 4 + s - 1
        full = part(n, 4 if s == 1 else (5 - s if k == 0 else 3 + s))
        if s == 1:
            if k == 0:
                sbuf[slot, :, 0:cut] = full[:, 0:cut].astype(BF)
            else:
                sbuf[slot, :, cut:width] = full[:, cut:width].astype(BF)
        elif s == 2 and k == 0:
            sbuf[slot, :, 0:cut] = (full[:, 0:cut] + rbuf[slot - 1, :, 0:cut].astype(F32)).astype(BF)
            sbuf[slot, :, cut:width] = full[:, cut:width].astype(BF)
        elif s == 2:
            sbuf[slot, :, 0:cut] = full[:, 0:cut].astype(BF)
            sbuf[slot, :, cut:width] = (full[:, cut:width] + rbuf[slot - 1, :, cut:width].astype(F32)).astype(BF)
        else:
            sbuf[slot, :, :] = (full + rbuf[slot - 1].astype(F32)).astype(BF)
        hop(n, k, s).start()

    def step(n, s):
        for k in range(2):
            hop(n, k, s - 1).wait_recv()
            begin(n, k, s)

    def leave(n):
        ret, lane0, width, _, _, _, at = legs[n]
        for g in range(NX):
            returned(n, g)

        def combine(i, carry):
            cols = pl.ds(pl.multiple_of(lax.rem(i + 2, 4) * MT, MT), MT)
            gu[cols, at:at + width] = mm(oh[:, cols], ret[:, lane0:lane0 + width], TN)
            return carry

        lax.fori_loop(0, 1, combine, 0)
        for k in range(2):
            begin(n, k, 1)
        lax.fori_loop(1, NZ * TOK // MT, combine, 0)

    def total(n):
        for k in range(2):
            hop(n, k, 4).wait_recv()
        rbuf = legs[n][5]
        return part(n, 0) + rbuf[3].astype(F32) + rbuf[7].astype(F32)

    pass_back(0, 3)

    @pl.when(core == 0)
    def _():
        own_grads()

    for g in FAR[:3]:
        pass_back(1, g)
    for g in FAR[:3]:
        pass_back(2, g)
    leave(0)
    step(0, 2)
    leave(1)
    step(0, 3)
    step(1, 2)
    leave(2)
    step(0, 4)
    step(1, 3)
    step(2, 2)

    @pl.when(core == 1)
    def _():
        own_grads()

    step(2, 3)
    step(1, 4)
    tot0 = total(0)
    gtok[:, 0:half] = tot0[:, 0:half].astype(BF)
    step(2, 4)
    share = jnp.transpose(tot0[:, half:wide])
    for j in range(topn):
        value = jnp.sum(jnp.where(row == ids_ref[j:j + 1, :], share, 0.0), axis=0, keepdims=True)
        ggate_ref[j:j + 1, :] = value / gates_ref[j:j + 1, :].astype(F32)
    tot1 = total(1)
    gtok[:, half:half + quarter] = tot1.astype(BF)
    tot2 = total(2)
    gtok[:, half + quarter:2 * half] = tot2.astype(BF)
    final = pltpu.make_async_copy(gtok, gtok_hbm, in_sem.at[3])
    final.start()

    for c in range(nchunk):
        for s in range(1, 5):
            for cp in gather_copies(c, s):
                cp.wait_send()
    for cp in wswap:
        cp.wait_send()
    for cp in tell:
        cp.wait_send()
    for c in range(nchunk):
        for g in range(NX):
            gone = send.at[chunks[c][0], pl.ds(g * GRP + MSG, GRP - MSG), lanes_of(c)]
            pltpu.make_async_copy(gone, gone, xs.at[c, g]).wait()
            if g > 0:
                along_y(c, g).wait_send()
    for n, (src, _, _, lane0, lanes) in enumerate(back_legs):
        for g in range(NX):
            gone = src.at[pl.ds(g * GRP + MSG, GRP - MSG), pl.ds(lane0, lanes)]
            pltpu.make_async_copy(gone, gone, bs.at[n, g]).wait()
            if g > 0:
                back_along_y(n, g).wait_send()
    gcopy.wait_send()
    dcopy.wait_send()
    for n in range(len(legs)):
        for s in range(1, 5):
            for k in range(2):
                hop(n, k, s).wait_send()
    for cp in outs:
        cp.wait()
    final.wait()


def finish(a0, a1, a2, a3, a4, o0, o1, o2, o3, o4, v0, v2, v3, v4, sem_in, sem_out):
    held = ((a0, v0, o0), (a2, v2, o2), (a3, v3, o3), (a4, v4, o4))
    ins = [pltpu.make_async_copy(a, v, sem_in.at[i]) for i, (a, v, _) in enumerate(held)]
    outs = [pltpu.make_async_copy(v, o, sem_out.at[i]) for i, (_, v, o) in enumerate(held)]
    for cp in ins:
        cp.start()
    o1[...] = a1[...].astype(BF)
    for cp, out in zip(ins, outs):
        cp.wait()
        out.start()
    for out in outs:
        out.wait()


def body(tokens, out_grad, expert_ids, gate_weights, keep_flags, gate_proj, up_proj, down_proj):
    width = tokens.shape[1]
    half = width // 2
    ff = gate_proj.shape[2]
    topn = expert_ids.shape[1]
    nexp = TOK
    wide = half + nexp
    any_spec = pl.BlockSpec(memory_space=pl.ANY)
    vmem = pl.BlockSpec(memory_space=pltpu.VMEM)
    dma = pltpu.SemaphoreType.DMA
    shapes = (
        jax.ShapeDtypeStruct(tokens.shape, BF),
        jax.ShapeDtypeStruct((topn, TOK), F32),
        jax.ShapeDtypeStruct(gate_proj.shape, BF),
        jax.ShapeDtypeStruct(up_proj.shape, BF),
        jax.ShapeDtypeStruct(down_proj.shape, BF),
    )
    scratch = [
        pltpu.VMEM((NZ * TOK, half), BF),
        pltpu.VMEM((NZ * TOK, half), BF),
        pltpu.VMEM((NZ * TOK, half), BF),
        pltpu.VMEM((NZ * TOK, half), BF),
        pltpu.VMEM((TOK, width), BF),
        pltpu.VMEM((NZ, 2 * topn, TOK), BF),
        pltpu.VMEM((PLANE, NZ * TOK), F32),
        pltpu.VMEM((PLANE, NZ * TOK), F32),
        pltpu.VMEM((SLOTS, NZ * TOK), BF),
        pltpu.VMEM((SLOTS, NZ * TOK), BF),
        pltpu.VMEM((4, SLOTS, half), BF),
        pltpu.VMEM((4, SLOTS - GRP, half), BF),
        pltpu.VMEM((4, SLOTS, half), BF),
        pltpu.VMEM((2, half, 2 * ff), BF),
        pltpu.VMEM((2, ff, half), BF),
        pltpu.VMEM((SLOTS, 2 * ff), F32),
        pltpu.VMEM((SLOTS, ff), F32),
        pltpu.VMEM((SLOTS, ff), BF),
        pltpu.VMEM((SLOTS, 2 * ff), BF),
        pltpu.VMEM((SLOTS, wide), BF),
        pltpu.VMEM((SLOTS, half), BF),
        pltpu.VMEM((SLOTS - GRP, wide), BF),
        pltpu.VMEM((SLOTS - GRP, half), BF),
        pltpu.VMEM((SLOTS, wide), BF),
        pltpu.VMEM((SLOTS, half), BF),
        pltpu.VMEM((8, TOK, wide), BF),
        pltpu.VMEM((8, TOK, wide), BF),
        pltpu.VMEM((8, TOK, half // 2), BF),
        pltpu.VMEM((8, TOK, half // 2), BF),
        pltpu.VMEM((8, TOK, half // 2), BF),
        pltpu.VMEM((8, TOK, half // 2), BF),
        pltpu.VMEM((half, 2 * ff), BF),
        pltpu.VMEM((ff, half), BF),
        pltpu.VMEM((half, 2 * ff), BF),
        pltpu.VMEM((ff, half), BF),
        pltpu.VMEM((half, 2 * ff), BF),
        pltpu.VMEM((ff, half), BF),
        pltpu.VMEM((TOK, width), BF),
        dma((4,)), dma((3,)), dma((3,)),
        dma((6, 2, 4)), dma((6, 2, 4)), dma((NZ,)), dma((NZ,)),
        dma((6, NX)), dma((6, NX)), dma((6, NX)), dma((6, NX)), dma((3, NX)), dma((3, NX)), dma((3, NX)), dma((3, NX)),
        dma((3, 8)), dma((3, 8)), dma((3,)), dma((3,)), dma((2,)), dma((2,)),
    ]
    done = pl.pallas_call(
        kernel,
        name="experts",
        out_shape=shapes,
        in_specs=[any_spec, any_spec, vmem, vmem, vmem, any_spec, any_spec, any_spec],
        out_specs=(any_spec, vmem, any_spec, any_spec, any_spec),
        scratch_shapes=scratch,
        compiler_params=pltpu.CompilerParams(
            collective_id=0, has_side_effects=True, vmem_limit_bytes=64 * 2**20 - 2**19
        ),
    )(tokens, out_grad, expert_ids.T, gate_weights.T, keep_flags.reshape(1, TOK), gate_proj, up_proj, down_proj)
    outs = pl.pallas_call(
        finish,
        name="finish",
        out_shape=(shapes[0], jax.ShapeDtypeStruct((topn, TOK), BF)) + shapes[2:],
        in_specs=[any_spec, vmem, any_spec, any_spec, any_spec],
        out_specs=(any_spec, vmem, any_spec, any_spec, any_spec),
        scratch_shapes=[pltpu.VMEM(shapes[i].shape, BF) for i in (0, 2, 3, 4)] + [dma((4,)), dma((4,))],
        compiler_params=pltpu.CompilerParams(vmem_limit_bytes=64 * 2**20 - 2**19),
    )(*done)
    return outs[0], outs[1].T, outs[2], outs[3], outs[4]


def solution(mesh):
    both = ("expert", "dp")
    in_specs = (
        P(both, None), P(both, None), P(both, None), P(both, None), P(both),
        P(both, None, None), P(both, None, None), P(both, None, None),
    )
    out_specs = (
        P(both, None), P(both, None), P(both, None, None), P(both, None, None), P(both, None, None),
    )
    return jax.shard_map(body, mesh=mesh, in_specs=in_specs, out_specs=out_specs, check_vma=False)
```

```python
import functools

import jax
import jax.numpy as jnp
from jax import lax
from jax.experimental import pallas as pl
from jax.experimental.pallas import tpu as pltpu
from jax.sharding import PartitionSpec as P

MESH = pl.DeviceIdType.MESH
BF = jnp.bfloat16
F32 = jnp.float32

TOK = 128
NZ = 8
NX = 4
CAP = 10
MSG = NZ * CAP
PLANE = NX * NX
SLOTS = PLANE * MSG
GRP = NX * MSG
FAR = (2, 1, 3, 0)
NN = (((1,), (0,)), ((), ()))
NT = (((1,), (1,)), ((), ()))
TN = (((0,), (0,)), ((), ()))


def mm(a, b, dims):
    return lax.dot_general(a, b, dims, preferred_element_type=F32)


def kernel(
    x_hbm, dy_hbm, ids_ref, gates_ref, keep_ref, wg_hbm, wu_hbm, wd_hbm,
    gtok_hbm, ggate_ref, ogg_hbm, ogu_hbm, ogd_hbm,
    ag0, ag1, ag2, ag3, dyraw, meta, told_out, told_in, pt, gt, oh, ohg, send, inter, recv, wgu, wd, gu, q, hid, dgu,
    ds0, ds1, rint0, rint1, ret0, ret1, rsa, rra, rsb, rrb, rsc, rrc, rsd, rrd, wsg, wsd, wrg, wrd, wog, wod, gtok,
    in_sem, w_sem, wout_sem,
    ags, agr, ms, mr, hs, hr, xs, xr, ys, yr, bs, br, cs, cr, rss, rsr, ws, wr, vs, vr,
):
    e = lax.axis_index("expert")
    d = lax.axis_index("dp")
    y, z = e // NZ, e % NZ
    x, core = d // 2, d % 2
    other = 1 - core

    def dev(dx, dy, dz):
        return (((y + dy + NX) % NX) * NZ + (z + dz + NZ) % NZ, ((x + dx + NX) % NX) * 2 + core)

    mate = (e, x * 2 + other)
    half = ag1.shape[1]
    hidn = hid.shape[1]
    nexp = TOK
    ags_bufs = [ag0, ag1, ag2, ag3]
    quarter = half // 2
    chunks = [(0, 0, quarter), (0, quarter, quarter), (1, 0, half), (2, 0, half), (3, 0, quarter), (3, quarter, quarter)]
    starts = [0, 0, 1, 3, 5, 6]
    nchunk = len(chunks)

    incp = [
        pltpu.make_async_copy(x_hbm.at[:, 0:half], ag0.at[0:TOK], in_sem.at[0]),
        pltpu.make_async_copy(x_hbm.at[:, half:2 * half], ag1.at[0:TOK], in_sem.at[1]),
        pltpu.make_async_copy(dy_hbm, dyraw, in_sem.at[2]),
    ]
    for cp in incp:
        cp.start()
    wl = [
        pltpu.make_async_copy(wg_hbm.at[0], wgu.at[core, :, 0:hidn], w_sem.at[0]),
        pltpu.make_async_copy(wu_hbm.at[0], wgu.at[core, :, hidn:2 * hidn], w_sem.at[1]),
        pltpu.make_async_copy(wd_hbm.at[0], wd.at[core], w_sem.at[2]),
    ]

    bar = pltpu.get_barrier_semaphore()
    for dz in range(1, NZ):
        pl.semaphore_signal(bar, inc=1, device_id=dev(0, 0, dz), device_id_type=MESH)
    pl.semaphore_signal(bar, inc=1, device_id=mate, device_id_type=MESH)
    for j in range(1, PLANE):
        pl.semaphore_signal(bar, inc=1, device_id=dev(j % NX, j // NX, 0), device_id_type=MESH)

    topn = ids_ref.shape[0]
    meta[0] = jnp.concatenate([ids_ref[...].astype(F32), gates_ref[...].astype(F32)], axis=0).astype(BF)
    pl.semaphore_wait(bar, PLANE - 1 + NZ)

    def remote(src, dst, s, r, to):
        return pltpu.make_async_remote_copy(
            src_ref=src, dst_ref=dst, send_sem=s, recv_sem=r, device_id=to, device_id_type=MESH
        )

    def block(k):
        return pl.ds(k * TOK, TOK)

    def gather_copies(c, s):
        buf, lane0, lanes = chunks[c]
        ag = ags_bufs[buf]
        a, b = (9 - s) % NZ, 8 - s
        lo = hi = pl.ds(lane0, lanes)
        if s == 4:
            if lanes > nexp:
                lo, hi = pl.ds(lane0, lanes // 2), pl.ds(lane0 + lanes // 2, lanes // 2)
        ways = [
            (ag.at[block(s - 1), lo], ag.at[block(s), lo], ags.at[c, 0, s - 1], agr.at[c, 0, s - 1], dev(0, 0, 1)),
            (ag.at[block(a), hi], ag.at[block(b), hi], ags.at[c, 1, s - 1], agr.at[c, 1, s - 1], dev(0, 0, -1)),
        ]
        return [remote(*way) for way in (ways[c:c + 1] if s == 4 and lanes == nexp else ways)]

    def ag_start(c):
        for cp in gather_copies(c, 1):
            cp.start()

    def ag_step(c, s):
        for cp in gather_copies(c, s):
            cp.wait_recv()
        if s < 4:
            for cp in gather_copies(c, s + 1):
                cp.start()

    tell = [remote(meta.at[0], meta.at[k], ms.at[k], mr.at[k], dev(0, 0, k)) for k in range(1, NZ)]
    for cp in tell:
        cp.start()
    incp[0].wait()
    for c in range(nchunk):
        if starts[c] == 0:
            ag_start(c)
    wswap = [
        remote(wg_hbm.at[0], wgu.at[core, :, 0:hidn], ws.at[0], wr.at[0], mate),
        remote(wu_hbm.at[0], wgu.at[core, :, hidn:2 * hidn], ws.at[1], wr.at[1], mate),
        remote(wd_hbm.at[0], wd.at[core], ws.at[2], wr.at[2], mate),
    ]
    wrecv = [
        remote(wg_hbm.at[0], wgu.at[other, :, 0:hidn], ws.at[0], wr.at[0], mate),
        remote(wu_hbm.at[0], wgu.at[other, :, hidn:2 * hidn], ws.at[1], wr.at[1], mate),
        remote(wd_hbm.at[0], wd.at[other], ws.at[2], wr.at[2], mate),
    ]

    row = lax.broadcasted_iota(jnp.int32, (TOK, TOK), 0)
    col = lax.broadcasted_iota(jnp.int32, (TOK, TOK), 1)
    row16 = lax.broadcasted_iota(jnp.int32, (PLANE, TOK), 0)
    wanted = (((y + row16 // NX) % NX) * (NZ * NX) + z * NX + (x + row16 % NX) % NX).astype(F32)
    earlier = jnp.where(row < col, 1.0, 0.0).astype(BF)
    col16 = lax.broadcasted_iota(jnp.int32, (PLANE, TOK), 1).astype(F32)
    pick = jnp.where(col16 == wanted, 1.0, 0.0).astype(BF)

    def route(r):
        told = meta[r].astype(F32)
        mine = jnp.zeros((PLANE, TOK), F32)
        weight = mine
        for j in range(topn):
            hit = wanted == told[j:j + 1, :]
            mine = jnp.where(hit, 1.0, mine)
            weight = jnp.where(hit, told[topn + j:topn + j + 1, :], weight)
        gt[:, r * TOK:(r + 1) * TOK] = weight
        place = mm(mine.astype(BF), earlier, NN)
        pt[:, r * TOK:(r + 1) * TOK] = jnp.where(mine > 0.5, place, -1.0)

    def mask_rows():
        incp[2].wait()
        keep = jnp.where(row == col, keep_ref[...].astype(F32), 0.0).astype(BF)
        ag2[0:TOK, :] = mm(keep, dyraw[:, 0:half], NN).astype(BF)
        ag3[0:TOK, :] = mm(keep, dyraw[:, half:2 * half], NN).astype(BF)

    prow = lax.broadcasted_iota(jnp.int32, (MSG, NZ * TOK), 0)
    pcol = lax.broadcasted_iota(jnp.int32, (MSG, NZ * TOK), 1)
    pattern = jnp.where(prow // CAP == pcol // TOK, prow % CAP, -2).astype(F32)

    def build(j, carry):
        rows = pl.ds(pl.multiple_of(j * MSG, MSG), MSG)
        oh[rows, :] = jnp.where(pattern == pt[pl.ds(j, 1), :], 1.0, 0.0).astype(BF)
        return carry

    def build_gated(j, carry):
        rows = pl.ds(pl.multiple_of(j * MSG, MSG), MSG)
        ohg[rows, :] = jnp.where(pattern == pt[pl.ds(j, 1), :], gt[pl.ds(j, 1), :], 0.0).astype(BF)
        return carry

    def rows_of(g):
        return pl.ds(pl.multiple_of(g * GRP, GRP), GRP)

    def lanes_of(c):
        return pl.ds(chunks[c][1], chunks[c][2])

    def hand_out(c, g):
        buf, at, width = chunks[c]
        sel = oh if buf < 2 else ohg
        res = mm(sel[g * GRP:(g + 1) * GRP, :], ags_bufs[buf][:, at:at + width], NN).astype(BF)
        target, base = (recv, 0) if g == 0 else (inter, (g - 1) * GRP)
        target[buf, base:base + MSG, at:at + width] = res[0:MSG]
        send[buf, g * GRP + MSG:(g + 1) * GRP, at:at + width] = res[MSG:]
        for dx in FAR[:3]:
            remote(send.at[buf, pl.ds(g * GRP + dx * MSG, MSG), lanes_of(c)],
                   target.at[buf, pl.ds(base + dx * MSG, MSG), lanes_of(c)],
                   xs.at[c, g], xr.at[c, g], dev(dx, 0, 0)).start()

    def along_y(c, g):
        buf = chunks[c][0]
        return remote(inter.at[buf, pl.ds((g - 1) * GRP, GRP), lanes_of(c)], recv.at[buf, pl.ds(g * GRP, GRP), lanes_of(c)],
                      ys.at[c, g], yr.at[c, g], dev(0, g, 0))

    def pass_on(c, g):
        came = inter.at[chunks[c][0], pl.ds((g - 1) * GRP + MSG, GRP - MSG), lanes_of(c)]
        pltpu.make_async_copy(came, came, xr.at[c, g]).wait()
        along_y(c, g).start()

    def landed(c, g):
        if g == 0:
            came = recv.at[chunks[c][0], pl.ds(MSG, GRP - MSG), lanes_of(c)]
            pltpu.make_async_copy(came, came, xr.at[c, 0]).wait()
        else:
            along_y(c, g).wait_recv()

    def tick(t, first=0, end=nchunk):
        for c in range(first, end):
            if 1 <= t - starts[c] <= 4:
                ag_step(c, t - starts[c])
        for c in range(first, end):
            if t == starts[c]:
                if c == 3:
                    mask_rows()
                ag_start(c)

    ag_step(0, 1)
    route(0)
    ag_step(1, 1)
    incp[1].wait()
    ag_start(2)
    ag_step(0, 2)
    for cp in tell:
        cp.wait_recv()
    for r in range(1, NZ):
        route(r)
    ag_step(1, 2)
    ag_step(0, 3)
    lax.fori_loop(0, PLANE, build, 0)
    ag_step(2, 1)
    ag_step(1, 3)
    ag_step(0, 4)

    def first_layer(h):
        for c in range(nchunk):
            if chunks[c][0] == h:
                for g in range(NX):
                    landed(c, g)

        def first(g, carry):
            part = mm(recv[h, rows_of(g), :], wgu[h], NN)
            if h == 0:
                gu[rows_of(g), :] = part
            else:
                gu[rows_of(g), :] = gu[rows_of(g), :] + part
            return carry

        lax.fori_loop(0, NX, first, 0)

    SUB = 32

    def activation(i, carry):
        rows = pl.ds(pl.multiple_of(i * SUB, SUB), SUB)
        gpre = gu[rows, 0:hidn]
        upre = gu[rows, hidn:2 * hidn]
        sig = jax.nn.sigmoid(gpre)
        swish = gpre * sig
        hid[rows, :] = (swish * upre).astype(BF)
        gu[rows, 0:hidn] = upre * sig * (1.0 + gpre * (1.0 - sig))
        gu[rows, hidn:2 * hidn] = swish
        return carry

    for c in range(nchunk):
        if c == 1:
            for cp in wl:
                cp.start()
            for cp in wswap:
                cp.start()
        if chunks[c][0] == 2:
            lax.fori_loop(0, PLANE, build_gated, 0)
        ahead = list(range(starts[c] + 5, starts[c + 1] + 5)) if c + 1 < nchunk else []
        for i, g in enumerate(FAR):
            hand_out(c, g)
            if c == 0 and i == 0:
                tick(3, 2)
            if c == 0 and i == 2:
                ag_step(1, 4)
                tick(4, 2)
            if c == nchunk - 2 and i == 0:
                for cp in wl:
                    cp.wait()
                for cp in wrecv:
                    cp.wait_recv()
                first_layer(0)
            if c == nchunk - 1 and i == 0:
                first_layer(1)
            if c == nchunk - 1 and i == 1:
                lax.fori_loop(0, SLOTS // SUB, activation, 0)
            if c > 0 and g > 0:
                pass_on(c - 1, g)
            if i < len(ahead) - 1:
                tick(ahead[i])
        for t in ahead[3:] if len(ahead) > 4 else ahead[-1:]:
            tick(t)

    for g in FAR[:3]:
        pass_on(nchunk - 1, g)

    for c in range(nchunk):
        for s in range(1, 5):
            for cp in gather_copies(c, s):
                cp.wait_send()

    def turn(m, carry):
        cols = pl.ds(pl.multiple_of(m * TOK, TOK), TOK)
        turned = jnp.transpose(oh[:, cols])
        ag0[cols, :] = turned[:, 0:half]
        ag1[cols, :] = turned[:, half:2 * half]
        ag2[cols, 0:SLOTS - 2 * half] = turned[:, 2 * half:SLOTS]
        return carry

    lax.fori_loop(0, NZ, turn, 0)

    for g in range(NX):
        landed(3, g)

    def back(g, carry):
        q[rows_of(g), :] = mm(recv[2, rows_of(g), :], wd[0], NT)
        return carry

    lax.fori_loop(0, NX, back, 0)

    expert_lane = y * (NZ * NX) + z * NX + x
    lane = lax.broadcasted_iota(jnp.int32, (SUB, TOK), 1)
    wide = half + nexp
    back_legs = [
        (ds0, rint0, ret0, 0, nexp + quarter),
        (ds0, rint0, ret0, nexp + quarter, quarter),
        (ds1, rint1, ret1, 0, quarter),
        (ds1, rint1, ret1, quarter, quarter),
    ]

    def send_back(n, g):
        src, mid, end, lane0, lanes = back_legs[n]
        target, base = (end, 0) if g == 0 else (mid, (g - 1) * GRP)
        for dx in FAR[:3]:
            remote(src.at[pl.ds(g * GRP + dx * MSG, MSG), pl.ds(lane0, lanes)],
                   target.at[pl.ds(base + dx * MSG, MSG), pl.ds(lane0, lanes)],
                   bs.at[n, g], br.at[n, g], dev(-dx, 0, 0)).start()

    def back_along_y(n, g):
        _, mid, end, lane0, lanes = back_legs[n]
        return remote(mid.at[pl.ds((g - 1) * GRP, GRP), pl.ds(lane0, lanes)],
                      end.at[pl.ds(g * GRP, GRP), pl.ds(lane0, lanes)], cs.at[n, g], cr.at[n, g], dev(0, -g, 0))

    def pass_back(n, g):
        _, mid, _, lane0, lanes = back_legs[n]
        came = mid.at[pl.ds((g - 1) * GRP + MSG, GRP - MSG), pl.ds(lane0, lanes)]
        pltpu.make_async_copy(came, came, br.at[n, g]).wait()
        back_along_y(n, g).start()

    def returned(n, g):
        _, _, end, lane0, lanes = back_legs[n]
        if g == 0:
            came = end.at[pl.ds(MSG, GRP - MSG), pl.ds(lane0, lanes)]
            pltpu.make_async_copy(came, came, br.at[n, 0]).wait()
        else:
            back_along_y(n, g).wait_recv()

    def keep_or_send(src, mid, end, g, lanes, value):
        target, base = (end, 0) if g == 0 else (mid, (g - 1) * GRP)
        target[base:base + MSG, lanes] = value[0:MSG]
        src[g * GRP + MSG:(g + 1) * GRP, lanes] = value[MSG:]

    def second(g):
        landed(4, g)
        landed(5, g)
        group = slice(g * GRP, (g + 1) * GRP)
        q[group, :] = q[group, :] + mm(recv[3, group, :], wd[1], NT)

        def grads(k, inner):
            rows = pl.ds(pl.multiple_of(g * GRP + k * SUB, SUB), SUB)
            dh = q[rows, :]
            dgu[rows, 0:hidn] = (dh * gu[rows, 0:hidn]).astype(BF)
            dgu[rows, hidn:2 * hidn] = (dh * gu[rows, hidn:2 * hidn]).astype(BF)
            dot = jnp.sum(dh * hid[rows, :].astype(F32), axis=1, keepdims=True)
            ds0[rows, 0:nexp] = jnp.where(lane == expert_lane, dot, 0.0).astype(BF)
            return inner

        lax.fori_loop(0, GRP // SUB, grads, 0)
        keep_or_send(ds0, rint0, ret0, g, slice(nexp, wide), mm(dgu[group, :], wgu[0], NT).astype(BF))
        target, base = (ret0, 0) if g == 0 else (rint0, (g - 1) * GRP)
        target[base:base + MSG, 0:nexp] = ds0[g * GRP:g * GRP + MSG, 0:nexp]
        if g > 0:
            send_back(0, g)

    def third(g):
        group = slice(g * GRP, (g + 1) * GRP)
        keep_or_send(ds1, rint1, ret1, g, slice(0, half), mm(dgu[group, :], wgu[1], NT).astype(BF))
        send_back(2, g)

    for g in (0, 2, 1, 3):
        second(g)
    send_back(0, 0)
    for g in FAR:
        send_back(1, g)
    third(2)
    third(1)
    pass_back(0, 2)
    third(3)
    pass_back(0, 1)
    third(0)
    pass_back(0, 3)
    for g in FAR:
        send_back(3, g)

    MT = 256

    def other_gu(m, carry):
        cols = pl.ds(pl.multiple_of(m * MT, MT), MT)
        wsg[cols, :] = mm(recv[other, :, cols], dgu[...], TN).astype(BF)
        return carry

    lax.fori_loop(0, half // MT, other_gu, 0)
    gcopy = remote(wsg, wrg, vs.at[0], vr.at[0], mate)
    gcopy.start()
    pass_back(1, 2)
    pass_back(1, 1)
    wsd[...] = mm(hid[...], recv[2 + other], TN).astype(BF)
    dcopy = remote(wsd, wrd, vs.at[1], vr.at[1], mate)
    dcopy.start()

    outs = [
        pltpu.make_async_copy(wog.at[:, 0:hidn], ogg_hbm.at[0], wout_sem.at[0]),
        pltpu.make_async_copy(wog.at[:, hidn:2 * hidn], ogu_hbm.at[0], wout_sem.at[1]),
        pltpu.make_async_copy(wod, ogd_hbm.at[0], wout_sem.at[2]),
    ]

    def own_gu(m, carry):
        cols = pl.ds(pl.multiple_of(m * MT, MT), MT)
        wog[cols, :] = (mm(recv[core, :, cols], dgu[...], TN) + wrg[cols, :].astype(F32)).astype(BF)
        return carry

    def own_grads():
        gcopy.wait_recv()
        lax.fori_loop(0, half // MT, own_gu, 0)
        outs[0].start()
        outs[1].start()
        dcopy.wait_recv()
        wod[...] = (mm(hid[...], recv[2 + core], TN) + wrd[...].astype(F32)).astype(BF)
        outs[2].start()

    legs = [
        (ret0, nexp, quarter, nexp, rsa, rra, 0),
        (ret0, nexp + quarter, quarter, nexp, rsb, rrb, quarter),
        (ret1, 0, quarter, nexp, rsc, rrc, half),
        (ret1, quarter, quarter, nexp, rsd, rrd, half + quarter),
    ]

    def part(n, r):
        width, at = legs[n][2], legs[n][6]
        return gu[r * TOK:(r + 1) * TOK, at:at + width]

    def hop(n, k, s):
        _, _, width, cut, sbuf, rbuf, _ = legs[n]
        lanes = pl.ds(0, width)
        if s == 1:
            lanes = pl.ds(0, cut) if k == 0 else pl.ds(cut, width - cut)
        slot = k * 4 + s - 1
        return remote(sbuf.at[slot, :, lanes], rbuf.at[slot, :, lanes], rss.at[n, slot], rsr.at[n, slot],
                      dev(0, 0, -1 if k == 0 else 1))

    def begin(n, k, s):
        _, _, width, cut, sbuf, rbuf, _ = legs[n]
        slot = k * 4 + s - 1
        full = part(n, 4 if s == 1 else (5 - s if k == 0 else 3 + s))
        if s == 1:
            if k == 0:
                sbuf[slot, :, 0:cut] = full[:, 0:cut].astype(BF)
            else:
                sbuf[slot, :, cut:width] = full[:, cut:width].astype(BF)
        elif s == 2 and k == 0:
            sbuf[slot, :, 0:cut] = (full[:, 0:cut] + rbuf[slot - 1, :, 0:cut].astype(F32)).astype(BF)
            sbuf[slot, :, cut:width] = full[:, cut:width].astype(BF)
        elif s == 2:
            sbuf[slot, :, 0:cut] = full[:, 0:cut].astype(BF)
            sbuf[slot, :, cut:width] = (full[:, cut:width] + rbuf[slot - 1, :, cut:width].astype(F32)).astype(BF)
        else:
            sbuf[slot, :, :] = (full + rbuf[slot - 1].astype(F32)).astype(BF)
        hop(n, k, s).start()

    def step(n, s):
        for k in range(2):
            hop(n, k, s - 1).wait_recv()
            begin(n, k, s)

    def select(cols, ret, came):
        return (
            mm(ag0[cols, :], ret[0:half, came], NN)
            + mm(ag1[cols, :], ret[half:2 * half, came], NN)
            + mm(ag2[cols, 0:SLOTS - 2 * half], ret[2 * half:SLOTS, came], NN)
        )

    def tell_home(r):
        return remote(told_out.at[r], told_in.at[r], hs.at[r], hr.at[r], dev(0, 0, -r))

    def gates_home():
        def turn_back(m, carry):
            cols = pl.ds(pl.multiple_of(m * MT, MT), MT)
            found = mm(pick, select(cols, ret0, slice(0, nexp)).astype(BF), NT).astype(BF)
            for r in range(MT // TOK):
                told_out[m * (MT // TOK) + r] = found[:, r * TOK:(r + 1) * TOK]
            return carry

        lax.fori_loop(0, NZ * TOK // MT, turn_back, 0)
        for r in range(1, NZ):
            tell_home(r).start()

    def leave(n):
        ret, lane0, width, _, _, _, at = legs[n]
        for g in range(NX):
            returned(n, g)

        def combine(i, carry):
            cols = pl.ds(pl.multiple_of(lax.rem(i + 2, 4) * MT, MT), MT)
            gu[cols, at:at + width] = select(cols, ret, slice(lane0, lane0 + width))
            return carry

        lax.fori_loop(0, 1, combine, 0)
        for k in range(2):
            begin(n, k, 1)
        lax.fori_loop(1, NZ * TOK // MT, combine, 0)

    def total(n):
        for k in range(2):
            hop(n, k, 4).wait_recv()
        rbuf = legs[n][5]
        return part(n, 0) + rbuf[3].astype(F32) + rbuf[7].astype(F32)

    pass_back(1, 3)

    leave(0)

    @pl.when(core == 0)
    def _():
        own_grads()

    for g in FAR[:3]:
        pass_back(2, g)
    step(0, 2)
    gates_home()
    for g in FAR[:3]:
        pass_back(3, g)
    leave(1)
    step(0, 3)
    step(1, 2)
    leave(2)
    step(0, 4)
    step(1, 3)
    step(2, 2)
    leave(3)
    step(1, 4)
    step(2, 3)
    step(3, 2)
    gtok[:, 0:quarter] = total(0).astype(BF)
    for r in range(1, NZ):
        tell_home(r).wait_recv()
    there = [told_out[0].astype(F32)] + [told_in[r].astype(F32) for r in range(1, NZ)]
    names = [((y + row16 // NX) % NX) * (NZ * NX) + ((z + r) % NZ) * NX + (x + row16 % NX) % NX for r in range(NZ)]
    for j in range(topn):
        value = jnp.zeros((PLANE, TOK), F32)
        for r in range(NZ):
            value = jnp.where(names[r] == ids_ref[j:j + 1, :], there[r], value)
        value = jnp.sum(value, axis=0, keepdims=True)
        ggate_ref[j:j + 1, :] = value / gates_ref[j:j + 1, :].astype(F32)

    @pl.when(core == 1)
    def _():
        own_grads()

    step(2, 4)
    step(3, 3)
    gtok[:, quarter:half] = total(1).astype(BF)
    step(3, 4)
    gtok[:, half:half + quarter] = total(2).astype(BF)
    gtok[:, half + quarter:2 * half] = total(3).astype(BF)
    final = pltpu.make_async_copy(gtok, gtok_hbm, in_sem.at[3])
    final.start()

    for cp in wswap:
        cp.wait_send()
    for cp in tell:
        cp.wait_send()
    for r in range(1, NZ):
        tell_home(r).wait_send()
    for c in range(nchunk):
        for g in range(NX):
            gone = send.at[chunks[c][0], pl.ds(g * GRP + MSG, GRP - MSG), lanes_of(c)]
            pltpu.make_async_copy(gone, gone, xs.at[c, g]).wait()
            if g > 0:
                along_y(c, g).wait_send()
    for n, (src, _, _, lane0, lanes) in enumerate(back_legs):
        for g in range(NX):
            gone = src.at[pl.ds(g * GRP + MSG, GRP - MSG), pl.ds(lane0, lanes)]
            pltpu.make_async_copy(gone, gone, bs.at[n, g]).wait()
            if g > 0:
                back_along_y(n, g).wait_send()
    gcopy.wait_send()
    dcopy.wait_send()
    for n in range(len(legs)):
        for s in range(1, 5):
            for k in range(2):
                hop(n, k, s).wait_send()
    for cp in outs:
        cp.wait()
    final.wait()


def finish(a0, a1, a2, a3, a4, o0, o1, o2, o3, o4, v0, v2, v3, v4, sem_in, sem_out):
    held = ((a0, v0, o0), (a2, v2, o2), (a3, v3, o3), (a4, v4, o4))
    ins = [pltpu.make_async_copy(a, v, sem_in.at[i]) for i, (a, v, _) in enumerate(held)]
    outs = [pltpu.make_async_copy(v, o, sem_out.at[i]) for i, (_, v, o) in enumerate(held)]
    for cp in ins:
        cp.start()
    o1[...] = a1[...].astype(BF)
    for cp, out in zip(ins, outs):
        cp.wait()
        out.start()
    for out in outs:
        out.wait()


def body(tokens, out_grad, expert_ids, gate_weights, keep_flags, gate_proj, up_proj, down_proj):
    width = tokens.shape[1]
    half = width // 2
    ff = gate_proj.shape[2]
    topn = expert_ids.shape[1]
    nexp = TOK
    wide = half + nexp
    any_spec = pl.BlockSpec(memory_space=pl.ANY)
    vmem = pl.BlockSpec(memory_space=pltpu.VMEM)
    dma = pltpu.SemaphoreType.DMA
    shapes = (
        jax.ShapeDtypeStruct(tokens.shape, BF),
        jax.ShapeDtypeStruct((topn, TOK), F32),
        jax.ShapeDtypeStruct(gate_proj.shape, BF),
        jax.ShapeDtypeStruct(up_proj.shape, BF),
        jax.ShapeDtypeStruct(down_proj.shape, BF),
    )
    scratch = [
        pltpu.VMEM((NZ * TOK, half), BF),
        pltpu.VMEM((NZ * TOK, half), BF),
        pltpu.VMEM((NZ * TOK, half), BF),
        pltpu.VMEM((NZ * TOK, half), BF),
        pltpu.VMEM((TOK, width), BF),
        pltpu.VMEM((NZ, 2 * topn, TOK), BF),
        pltpu.VMEM((NZ, PLANE, TOK), BF),
        pltpu.VMEM((NZ, PLANE, TOK), BF),
        pltpu.VMEM((PLANE, NZ * TOK), F32),
        pltpu.VMEM((PLANE, NZ * TOK), F32),
        pltpu.VMEM((SLOTS, NZ * TOK), BF),
        pltpu.VMEM((SLOTS, NZ * TOK), BF),
        pltpu.VMEM((4, SLOTS, half), BF),
        pltpu.VMEM((4, SLOTS - GRP, half), BF),
        pltpu.VMEM((4, SLOTS, half), BF),
        pltpu.VMEM((2, half, 2 * ff), BF),
        pltpu.VMEM((2, ff, half), BF),
        pltpu.VMEM((SLOTS, 2 * ff), F32),
        pltpu.VMEM((SLOTS, ff), F32),
        pltpu.VMEM((SLOTS, ff), BF),
        pltpu.VMEM((SLOTS, 2 * ff), BF),
        pltpu.VMEM((SLOTS, wide), BF),
        pltpu.VMEM((SLOTS, half), BF),
        pltpu.VMEM((SLOTS - GRP, wide), BF),
        pltpu.VMEM((SLOTS - GRP, half), BF),
        pltpu.VMEM((SLOTS, wide), BF),
        pltpu.VMEM((SLOTS, half), BF),
        pltpu.VMEM((8, TOK, half // 2), BF),
        pltpu.VMEM((8, TOK, half // 2), BF),
        pltpu.VMEM((8, TOK, half // 2), BF),
        pltpu.VMEM((8, TOK, half // 2), BF),
        pltpu.VMEM((8, TOK, half // 2), BF),
        pltpu.VMEM((8, TOK, half // 2), BF),
        pltpu.VMEM((8, TOK, half // 2), BF),
        pltpu.VMEM((8, TOK, half // 2), BF),
        pltpu.VMEM((half, 2 * ff), BF),
        pltpu.VMEM((ff, half), BF),
        pltpu.VMEM((half, 2 * ff), BF),
        pltpu.VMEM((ff, half), BF),
        pltpu.VMEM((half, 2 * ff), BF),
        pltpu.VMEM((ff, half), BF),
        pltpu.VMEM((TOK, width), BF),
        dma((4,)), dma((3,)), dma((3,)),
        dma((6, 2, 4)), dma((6, 2, 4)), dma((NZ,)), dma((NZ,)), dma((NZ,)), dma((NZ,)),
        dma((6, NX)), dma((6, NX)), dma((6, NX)), dma((6, NX)), dma((4, NX)), dma((4, NX)), dma((4, NX)), dma((4, NX)),
        dma((4, 8)), dma((4, 8)), dma((3,)), dma((3,)), dma((2,)), dma((2,)),
    ]
    done = pl.pallas_call(
        kernel,
        name="experts",
        out_shape=shapes,
        in_specs=[any_spec, any_spec, vmem, vmem, vmem, any_spec, any_spec, any_spec],
        out_specs=(any_spec, vmem, any_spec, any_spec, any_spec),
        scratch_shapes=scratch,
        compiler_params=pltpu.CompilerParams(
            collective_id=0, has_side_effects=True, vmem_limit_bytes=64 * 2**20 - 2**19
        ),
    )(tokens, out_grad, expert_ids.T, gate_weights.T, keep_flags.reshape(1, TOK), gate_proj, up_proj, down_proj)
    outs = pl.pallas_call(
        finish,
        name="finish",
        out_shape=(shapes[0], jax.ShapeDtypeStruct((topn, TOK), BF)) + shapes[2:],
        in_specs=[any_spec, vmem, any_spec, any_spec, any_spec],
        out_specs=(any_spec, vmem, any_spec, any_spec, any_spec),
        scratch_shapes=[pltpu.VMEM(shapes[i].shape, BF) for i in (0, 2, 3, 4)] + [dma((4,)), dma((4,))],
        compiler_params=pltpu.CompilerParams(vmem_limit_bytes=64 * 2**20 - 2**19),
    )(*done)
    return outs[0], outs[1].T, outs[2], outs[3], outs[4]


def solution(mesh):
    both = ("expert", "dp")
    in_specs = (
        P(both, None), P(both, None), P(both, None), P(both, None), P(both),
        P(both, None, None), P(both, None, None), P(both, None, None),
    )
    out_specs = (
        P(both, None), P(both, None), P(both, None, None), P(both, None, None), P(both, None, None),
    )
    return jax.shard_map(body, mesh=mesh, in_specs=in_specs, out_specs=out_specs, check_vma=False)
```

```python
import functools

import jax
import jax.numpy as jnp
from jax import lax
from jax.experimental import pallas as pl
from jax.experimental.pallas import tpu as pltpu
from jax.sharding import PartitionSpec as P

MESH = pl.DeviceIdType.MESH
BF = jnp.bfloat16
F32 = jnp.float32

TOK = 128
NZ = 8
NX = 4
CAP = 10
MSG = NZ * CAP
PLANE = NX * NX
SLOTS = PLANE * MSG
GRP = NX * MSG
FAR = (2, 1, 3, 0)
NN = (((1,), (0,)), ((), ()))
NT = (((1,), (1,)), ((), ()))
TN = (((0,), (0,)), ((), ()))


def mm(a, b, dims):
    return lax.dot_general(a, b, dims, preferred_element_type=F32)


def kernel(
    x_hbm, dy_hbm, ids_ref, gates_ref, keep_ref, wg_hbm, wu_hbm, wd_hbm,
    gtok_hbm, ggate_ref, ogg_hbm, ogu_hbm, ogd_hbm,
    ag0, ag1, ag2, ag3, dyraw, meta, told_out, told_in, pt, gt, oh, ohg, send, inter, recv, wgu, wd, gu, q, hid, dgu,
    ds0, ds1, rint0, rint1, ret0, ret1, rsa, rra, rsb, rrb, rsc, rrc, rsd, rrd, wsg, wsd, wrg, wrd, wog, wod, gtok,
    in_sem, w_sem, wout_sem,
    ags, agr, ms, mr, hs, hr, xs, xr, ys, yr, bs, br, cs, cr, rss, rsr, ws, wr, vs, vr,
):
    e = lax.axis_index("expert")
    d = lax.axis_index("dp")
    y, z = e // NZ, e % NZ
    x, core = d // 2, d % 2
    other = 1 - core

    def dev(dx, dy, dz):
        return (((y + dy + NX) % NX) * NZ + (z + dz + NZ) % NZ, ((x + dx + NX) % NX) * 2 + core)

    mate = (e, x * 2 + other)
    half = ag1.shape[1]
    hidn = hid.shape[1]
    nexp = TOK
    ags_bufs = [ag0, ag1, ag2, ag3]
    quarter = half // 2
    chunks = [(0, 0, quarter), (0, quarter, quarter), (1, 0, half), (2, 0, half), (3, 0, quarter), (3, quarter, quarter)]
    starts = [0, 0, 1, 3, 5, 6]
    nchunk = len(chunks)

    incp = [
        pltpu.make_async_copy(x_hbm.at[:, 0:half], ag0.at[0:TOK], in_sem.at[0]),
        pltpu.make_async_copy(x_hbm.at[:, half:2 * half], ag1.at[0:TOK], in_sem.at[1]),
        pltpu.make_async_copy(dy_hbm, dyraw, in_sem.at[2]),
    ]
    for cp in incp:
        cp.start()
    wl = [
        pltpu.make_async_copy(wg_hbm.at[0], wgu.at[core, :, 0:hidn], w_sem.at[0]),
        pltpu.make_async_copy(wu_hbm.at[0], wgu.at[core, :, hidn:2 * hidn], w_sem.at[1]),
        pltpu.make_async_copy(wd_hbm.at[0], wd.at[core], w_sem.at[2]),
    ]

    bar = pltpu.get_barrier_semaphore()
    for dz in range(1, NZ):
        pl.semaphore_signal(bar, inc=1, device_id=dev(0, 0, dz), device_id_type=MESH)
    pl.semaphore_signal(bar, inc=1, device_id=mate, device_id_type=MESH)
    for k in range(1, NX):
        pl.semaphore_signal(bar, inc=1, device_id=dev(k, 0, 0), device_id_type=MESH)
        pl.semaphore_signal(bar, inc=1, device_id=dev(0, k, 0), device_id_type=MESH)

    topn = ids_ref.shape[0]
    meta[0] = jnp.concatenate([ids_ref[...].astype(F32), gates_ref[...].astype(F32)], axis=0).astype(BF)
    pl.semaphore_wait(bar, 2 * (NX - 1) + NZ)

    def remote(src, dst, s, r, to):
        return pltpu.make_async_remote_copy(
            src_ref=src, dst_ref=dst, send_sem=s, recv_sem=r, device_id=to, device_id_type=MESH
        )

    def block(k):
        return pl.ds(k * TOK, TOK)

    def gather_copies(c, s):
        buf, lane0, lanes = chunks[c]
        ag = ags_bufs[buf]
        a, b = (9 - s) % NZ, 8 - s
        lo = hi = pl.ds(lane0, lanes)
        if s == 4:
            if lanes > nexp:
                lo, hi = pl.ds(lane0, lanes // 2), pl.ds(lane0 + lanes // 2, lanes // 2)
        ways = [
            (ag.at[block(s - 1), lo], ag.at[block(s), lo], ags.at[c, 0, s - 1], agr.at[c, 0, s - 1], dev(0, 0, 1)),
            (ag.at[block(a), hi], ag.at[block(b), hi], ags.at[c, 1, s - 1], agr.at[c, 1, s - 1], dev(0, 0, -1)),
        ]
        return [remote(*way) for way in (ways[c:c + 1] if s == 4 and lanes == nexp else ways)]

    def ag_start(c):
        for cp in gather_copies(c, 1):
            cp.start()

    def ag_step(c, s):
        for cp in gather_copies(c, s):
            cp.wait_recv()
        if s < 4:
            for cp in gather_copies(c, s + 1):
                cp.start()

    tell = [remote(meta.at[0], meta.at[k], ms.at[k], mr.at[k], dev(0, 0, k)) for k in range(1, NZ)]
    for cp in tell:
        cp.start()
    incp[0].wait()
    for c in range(nchunk):
        if starts[c] == 0:
            ag_start(c)
    wswap = [
        remote(wg_hbm.at[0], wgu.at[core, :, 0:hidn], ws.at[0], wr.at[0], mate),
        remote(wu_hbm.at[0], wgu.at[core, :, hidn:2 * hidn], ws.at[1], wr.at[1], mate),
        remote(wd_hbm.at[0], wd.at[core], ws.at[2], wr.at[2], mate),
    ]
    wrecv = [
        remote(wg_hbm.at[0], wgu.at[other, :, 0:hidn], ws.at[0], wr.at[0], mate),
        remote(wu_hbm.at[0], wgu.at[other, :, hidn:2 * hidn], ws.at[1], wr.at[1], mate),
        remote(wd_hbm.at[0], wd.at[other], ws.at[2], wr.at[2], mate),
    ]

    row = lax.broadcasted_iota(jnp.int32, (TOK, TOK), 0)
    col = lax.broadcasted_iota(jnp.int32, (TOK, TOK), 1)
    row16 = lax.broadcasted_iota(jnp.int32, (PLANE, TOK), 0)
    wanted = (((y + row16 // NX) % NX) * (NZ * NX) + z * NX + (x + row16 % NX) % NX).astype(F32)
    earlier = jnp.where(row < col, 1.0, 0.0).astype(BF)
    col16 = lax.broadcasted_iota(jnp.int32, (PLANE, TOK), 1).astype(F32)
    pick = jnp.where(col16 == wanted, 1.0, 0.0).astype(BF)

    def route(r):
        told = meta[r].astype(F32)
        mine = jnp.zeros((PLANE, TOK), F32)
        weight = mine
        for j in range(topn):
            hit = wanted == told[j:j + 1, :]
            mine = jnp.where(hit, 1.0, mine)
            weight = jnp.where(hit, told[topn + j:topn + j + 1, :], weight)
        gt[:, r * TOK:(r + 1) * TOK] = weight
        place = mm(mine.astype(BF), earlier, NN)
        pt[:, r * TOK:(r + 1) * TOK] = jnp.where(mine > 0.5, place, -1.0)

    def mask_rows():
        incp[2].wait()
        keep = jnp.where(row == col, keep_ref[...].astype(F32), 0.0).astype(BF)
        ag2[0:TOK, :] = mm(keep, dyraw[:, 0:half], NN).astype(BF)
        ag3[0:TOK, :] = mm(keep, dyraw[:, half:2 * half], NN).astype(BF)

    prow = lax.broadcasted_iota(jnp.int32, (MSG, NZ * TOK), 0)
    pcol = lax.broadcasted_iota(jnp.int32, (MSG, NZ * TOK), 1)
    pattern = jnp.where(prow // CAP == pcol // TOK, prow % CAP, -2).astype(F32)

    def build(j, carry):
        rows = pl.ds(pl.multiple_of(j * MSG, MSG), MSG)
        oh[rows, :] = jnp.where(pattern == pt[pl.ds(j, 1), :], 1.0, 0.0).astype(BF)
        return carry

    def build_gated(j, carry):
        rows = pl.ds(pl.multiple_of(j * MSG, MSG), MSG)
        ohg[rows, :] = jnp.where(pattern == pt[pl.ds(j, 1), :], gt[pl.ds(j, 1), :], 0.0).astype(BF)
        return carry

    def rows_of(g):
        return pl.ds(pl.multiple_of(g * GRP, GRP), GRP)

    def lanes_of(c):
        return pl.ds(chunks[c][1], chunks[c][2])

    def hand_out(c, g):
        buf, at, width = chunks[c]
        sel = oh if buf < 2 else ohg
        res = mm(sel[g * GRP:(g + 1) * GRP, :], ags_bufs[buf][:, at:at + width], NN).astype(BF)
        target, base = (recv, 0) if g == 0 else (inter, (g - 1) * GRP)
        target[buf, base:base + MSG, at:at + width] = res[0:MSG]
        send[buf, g * GRP + MSG:(g + 1) * GRP, at:at + width] = res[MSG:]
        for dx in FAR[:3]:
            remote(send.at[buf, pl.ds(g * GRP + dx * MSG, MSG), lanes_of(c)],
                   target.at[buf, pl.ds(base + dx * MSG, MSG), lanes_of(c)],
                   xs.at[c, g], xr.at[c, g], dev(dx, 0, 0)).start()

    def along_y(c, g):
        buf = chunks[c][0]
        return remote(inter.at[buf, pl.ds((g - 1) * GRP, GRP), lanes_of(c)], recv.at[buf, pl.ds(g * GRP, GRP), lanes_of(c)],
                      ys.at[c, g], yr.at[c, g], dev(0, g, 0))

    def pass_on(c, g):
        came = inter.at[chunks[c][0], pl.ds((g - 1) * GRP + MSG, GRP - MSG), lanes_of(c)]
        pltpu.make_async_copy(came, came, xr.at[c, g]).wait()
        along_y(c, g).start()

    def landed(c, g):
        if g == 0:
            came = recv.at[chunks[c][0], pl.ds(MSG, GRP - MSG), lanes_of(c)]
            pltpu.make_async_copy(came, came, xr.at[c, 0]).wait()
        else:
            along_y(c, g).wait_recv()

    def tick(t, first=0, end=nchunk):
        for c in range(first, end):
            if 1 <= t - starts[c] <= 4:
                ag_step(c, t - starts[c])
        for c in range(first, end):
            if t == starts[c]:
                if c == 3:
                    mask_rows()
                ag_start(c)

    ag_step(0, 1)
    route(0)
    ag_step(1, 1)
    incp[1].wait()
    ag_start(2)
    ag_step(0, 2)
    for cp in tell:
        cp.wait_recv()
    for r in range(1, NZ):
        route(r)
    ag_step(1, 2)
    ag_step(0, 3)
    lax.fori_loop(0, PLANE, build, 0)
    ag_step(2, 1)
    ag_step(1, 3)
    ag_step(0, 4)

    def first_layer(h):
        for c in range(nchunk):
            if chunks[c][0] == h:
                for g in range(NX):
                    landed(c, g)

        def first(g, carry):
            part = mm(recv[h, rows_of(g), :], wgu[h], NN)
            if h == 0:
                gu[rows_of(g), :] = part
            else:
                gu[rows_of(g), :] = gu[rows_of(g), :] + part
            return carry

        lax.fori_loop(0, NX, first, 0)

    SUB = 32

    def activation(i, carry):
        rows = pl.ds(pl.multiple_of(i * SUB, SUB), SUB)
        gpre = gu[rows, 0:hidn]
        upre = gu[rows, hidn:2 * hidn]
        sig = jax.nn.sigmoid(gpre)
        swish = gpre * sig
        hid[rows, :] = (swish * upre).astype(BF)
        gu[rows, 0:hidn] = upre * sig * (1.0 + gpre * (1.0 - sig))
        gu[rows, hidn:2 * hidn] = swish
        return carry

    for c in range(nchunk):
        if c == 1:
            for cp in wl:
                cp.start()
            for cp in wswap:
                cp.start()
        if chunks[c][0] == 2:
            lax.fori_loop(0, PLANE, build_gated, 0)
        ahead = list(range(starts[c] + 5, starts[c + 1] + 5)) if c + 1 < nchunk else []
        for i, g in enumerate(FAR):
            hand_out(c, g)
            if c == 0 and i == 0:
                tick(3, 2)
            if c == 0 and i == 2:
                ag_step(1, 4)
                tick(4, 2)
            if c == nchunk - 2 and i == 0:
                for cp in wl:
                    cp.wait()
                for cp in wrecv:
                    cp.wait_recv()
                first_layer(0)
            if c == nchunk - 1 and i == 0:
                first_layer(1)
            if c == nchunk - 1 and i == 1:
                lax.fori_loop(0, SLOTS // SUB, activation, 0)
            if c > 0 and g > 0:
                pass_on(c - 1, g)
            if i < len(ahead) - 1:
                tick(ahead[i])
        for t in ahead[3:] if len(ahead) > 4 else ahead[-1:]:
            tick(t)

    for g in FAR[:3]:
        pass_on(nchunk - 1, g)

    for c in range(nchunk):
        for s in range(1, 5):
            for cp in gather_copies(c, s):
                cp.wait_send()

    def turn(m, carry):
        cols = pl.ds(pl.multiple_of(m * TOK, TOK), TOK)
        turned = jnp.transpose(oh[:, cols])
        ag0[cols, :] = turned[:, 0:half]
        ag1[cols, :] = turned[:, half:2 * half]
        ag2[cols, 0:SLOTS - 2 * half] = turned[:, 2 * half:SLOTS]
        return carry

    lax.fori_loop(0, NZ, turn, 0)

    for g in range(NX):
        landed(3, g)

    def back(g, carry):
        q[rows_of(g), :] = mm(recv[2, rows_of(g), :], wd[0], NT)
        return carry

    lax.fori_loop(0, NX, back, 0)

    expert_lane = y * (NZ * NX) + z * NX + x
    lane = lax.broadcasted_iota(jnp.int32, (SUB, TOK), 1)
    wide = half + nexp
    back_legs = [
        (ds0, rint0, ret0, 0, nexp + quarter),
        (ds0, rint0, ret0, nexp + quarter, quarter),
        (ds1, rint1, ret1, 0, quarter),
        (ds1, rint1, ret1, quarter, quarter),
    ]

    def send_back(n, g):
        src, mid, end, lane0, lanes = back_legs[n]
        target, base = (end, 0) if g == 0 else (mid, (g - 1) * GRP)
        for dx in FAR[:3]:
            remote(src.at[pl.ds(g * GRP + dx * MSG, MSG), pl.ds(lane0, lanes)],
                   target.at[pl.ds(base + dx * MSG, MSG), pl.ds(lane0, lanes)],
                   bs.at[n, g], br.at[n, g], dev(-dx, 0, 0)).start()

    def back_along_y(n, g):
        _, mid, end, lane0, lanes = back_legs[n]
        return remote(mid.at[pl.ds((g - 1) * GRP, GRP), pl.ds(lane0, lanes)],
                      end.at[pl.ds(g * GRP, GRP), pl.ds(lane0, lanes)], cs.at[n, g], cr.at[n, g], dev(0, -g, 0))

    def pass_back(n, g):
        _, mid, _, lane0, lanes = back_legs[n]
        came = mid.at[pl.ds((g - 1) * GRP + MSG, GRP - MSG), pl.ds(lane0, lanes)]
        pltpu.make_async_copy(came, came, br.at[n, g]).wait()
        back_along_y(n, g).start()

    def returned(n, g):
        _, _, end, lane0, lanes = back_legs[n]
        if g == 0:
            came = end.at[pl.ds(MSG, GRP - MSG), pl.ds(lane0, lanes)]
            pltpu.make_async_copy(came, came, br.at[n, 0]).wait()
        else:
            back_along_y(n, g).wait_recv()

    def keep_or_send(src, mid, end, g, lanes, value):
        target, base = (end, 0) if g == 0 else (mid, (g - 1) * GRP)
        target[base:base + MSG, lanes] = value[0:MSG]
        src[g * GRP + MSG:(g + 1) * GRP, lanes] = value[MSG:]

    def second(g):
        landed(4, g)
        landed(5, g)
        group = slice(g * GRP, (g + 1) * GRP)
        q[group, :] = q[group, :] + mm(recv[3, group, :], wd[1], NT)

        def grads(k, inner):
            rows = pl.ds(pl.multiple_of(g * GRP + k * SUB, SUB), SUB)
            dh = q[rows, :]
            dgu[rows, 0:hidn] = (dh * gu[rows, 0:hidn]).astype(BF)
            dgu[rows, hidn:2 * hidn] = (dh * gu[rows, hidn:2 * hidn]).astype(BF)
            dot = jnp.sum(dh * hid[rows, :].astype(F32), axis=1, keepdims=True)
            ds0[rows, 0:nexp] = jnp.where(lane == expert_lane, dot, 0.0).astype(BF)
            return inner

        lax.fori_loop(0, GRP // SUB, grads, 0)
        keep_or_send(ds0, rint0, ret0, g, slice(nexp, wide), mm(dgu[group, :], wgu[0], NT).astype(BF))
        target, base = (ret0, 0) if g == 0 else (rint0, (g - 1) * GRP)
        target[base:base + MSG, 0:nexp] = ds0[g * GRP:g * GRP + MSG, 0:nexp]
        if g > 0:
            send_back(0, g)

    def third(g):
        group = slice(g * GRP, (g + 1) * GRP)
        keep_or_send(ds1, rint1, ret1, g, slice(0, half), mm(dgu[group, :], wgu[1], NT).astype(BF))
        send_back(2, g)

    for g in (0, 2, 1, 3):
        second(g)
    send_back(0, 0)
    for g in FAR:
        send_back(1, g)
    third(2)
    third(1)
    pass_back(0, 2)
    third(3)
    pass_back(0, 1)
    third(0)
    pass_back(0, 3)
    for g in FAR:
        send_back(3, g)

    MT = 256

    def other_gu(m, carry):
        cols = pl.ds(pl.multiple_of(m * MT, MT), MT)
        wsg[cols, :] = mm(recv[other, :, cols], dgu[...], TN).astype(BF)
        return carry

    lax.fori_loop(0, half // MT, other_gu, 0)
    gcopy = remote(wsg, wrg, vs.at[0], vr.at[0], mate)
    gcopy.start()
    pass_back(1, 2)
    pass_back(1, 1)
    wsd[...] = mm(hid[...], recv[2 + other], TN).astype(BF)
    dcopy = remote(wsd, wrd, vs.at[1], vr.at[1], mate)
    dcopy.start()

    outs = [
        pltpu.make_async_copy(wog.at[:, 0:hidn], ogg_hbm.at[0], wout_sem.at[0]),
        pltpu.make_async_copy(wog.at[:, hidn:2 * hidn], ogu_hbm.at[0], wout_sem.at[1]),
        pltpu.make_async_copy(wod, ogd_hbm.at[0], wout_sem.at[2]),
    ]

    def own_gu(m, carry):
        cols = pl.ds(pl.multiple_of(m * MT, MT), MT)
        wog[cols, :] = (mm(recv[core, :, cols], dgu[...], TN) + wrg[cols, :].astype(F32)).astype(BF)
        return carry

    def own_grads():
        gcopy.wait_recv()
        lax.fori_loop(0, half // MT, own_gu, 0)
        outs[0].start()
        outs[1].start()
        dcopy.wait_recv()
        wod[...] = (mm(hid[...], recv[2 + core], TN) + wrd[...].astype(F32)).astype(BF)
        outs[2].start()

    legs = [
        (ret0, nexp, quarter, nexp, rsa, rra, 0),
        (ret0, nexp + quarter, quarter, nexp, rsb, rrb, quarter),
        (ret1, 0, quarter, nexp, rsc, rrc, half),
        (ret1, quarter, quarter, nexp, rsd, rrd, half + quarter),
    ]

    def part(n, r):
        width, at = legs[n][2], legs[n][6]
        return gu[r * TOK:(r + 1) * TOK, at:at + width]

    def hop(n, k, s):
        _, _, width, cut, sbuf, rbuf, _ = legs[n]
        lanes = pl.ds(0, width)
        if s == 1:
            lanes = pl.ds(0, cut) if k == 0 else pl.ds(cut, width - cut)
        slot = k * 4 + s - 1
        return remote(sbuf.at[slot, :, lanes], rbuf.at[slot, :, lanes], rss.at[n, slot], rsr.at[n, slot],
                      dev(0, 0, -1 if k == 0 else 1))

    def begin(n, k, s):
        _, _, width, cut, sbuf, rbuf, _ = legs[n]
        slot = k * 4 + s - 1
        full = part(n, 4 if s == 1 else (5 - s if k == 0 else 3 + s))
        if s == 1:
            if k == 0:
                sbuf[slot, :, 0:cut] = full[:, 0:cut].astype(BF)
            else:
                sbuf[slot, :, cut:width] = full[:, cut:width].astype(BF)
        elif s == 2 and k == 0:
            sbuf[slot, :, 0:cut] = (full[:, 0:cut] + rbuf[slot - 1, :, 0:cut].astype(F32)).astype(BF)
            sbuf[slot, :, cut:width] = full[:, cut:width].astype(BF)
        elif s == 2:
            sbuf[slot, :, 0:cut] = full[:, 0:cut].astype(BF)
            sbuf[slot, :, cut:width] = (full[:, cut:width] + rbuf[slot - 1, :, cut:width].astype(F32)).astype(BF)
        else:
            sbuf[slot, :, :] = (full + rbuf[slot - 1].astype(F32)).astype(BF)
        hop(n, k, s).start()

    def step(n, s):
        for k in range(2):
            hop(n, k, s - 1).wait_recv()
            begin(n, k, s)

    def select(cols, ret, came):
        return (
            mm(ag0[cols, :], ret[0:half, came], NN)
            + mm(ag1[cols, :], ret[half:2 * half, came], NN)
            + mm(ag2[cols, 0:SLOTS - 2 * half], ret[2 * half:SLOTS, came], NN)
        )

    def tell_home(r):
        return remote(told_out.at[r], told_in.at[r], hs.at[r], hr.at[r], dev(0, 0, -r))

    def gates_home():
        def turn_back(m, carry):
            cols = pl.ds(pl.multiple_of(m * MT, MT), MT)
            found = mm(pick, select(cols, ret0, slice(0, nexp)).astype(BF), NT).astype(BF)
            for r in range(MT // TOK):
                told_out[m * (MT // TOK) + r] = found[:, r * TOK:(r + 1) * TOK]
            return carry

        lax.fori_loop(0, NZ * TOK // MT, turn_back, 0)
        for r in range(1, NZ):
            tell_home(r).start()

    def leave(n):
        ret, lane0, width, _, _, _, at = legs[n]
        for g in range(NX):
            returned(n, g)

        def combine(i, carry):
            cols = pl.ds(pl.multiple_of(lax.rem(i + 2, 4) * MT, MT), MT)
            gu[cols, at:at + width] = select(cols, ret, slice(lane0, lane0 + width))
            return carry

        lax.fori_loop(0, 1, combine, 0)
        for k in range(2):
            begin(n, k, 1)
        lax.fori_loop(1, NZ * TOK // MT, combine, 0)

    def total(n):
        for k in range(2):
            hop(n, k, 4).wait_recv()
        rbuf = legs[n][5]
        return part(n, 0) + rbuf[3].astype(F32) + rbuf[7].astype(F32)

    pass_back(1, 3)

    leave(0)

    @pl.when(core == 0)
    def _():
        own_grads()

    for g in FAR[:3]:
        pass_back(2, g)
    step(0, 2)
    gates_home()
    for g in FAR[:3]:
        pass_back(3, g)
    leave(1)
    step(0, 3)
    step(1, 2)
    leave(2)
    step(0, 4)
    step(1, 3)
    step(2, 2)
    leave(3)
    step(1, 4)
    step(2, 3)
    step(3, 2)
    gtok[:, 0:quarter] = total(0).astype(BF)
    for r in range(1, NZ):
        tell_home(r).wait_recv()
    there = [told_out[0].astype(F32)] + [told_in[r].astype(F32) for r in range(1, NZ)]
    names = [((y + row16 // NX) % NX) * (NZ * NX) + ((z + r) % NZ) * NX + (x + row16 % NX) % NX for r in range(NZ)]
    for j in range(topn):
        value = jnp.zeros((PLANE, TOK), F32)
        for r in range(NZ):
            value = jnp.where(names[r] == ids_ref[j:j + 1, :], there[r], value)
        value = jnp.sum(value, axis=0, keepdims=True)
        ggate_ref[j:j + 1, :] = value / gates_ref[j:j + 1, :].astype(F32)

    @pl.when(core == 1)
    def _():
        own_grads()

    step(2, 4)
    step(3, 3)
    gtok[:, quarter:half] = total(1).astype(BF)
    step(3, 4)
    gtok[:, half:half + quarter] = total(2).astype(BF)
    gtok[:, half + quarter:2 * half] = total(3).astype(BF)
    final = pltpu.make_async_copy(gtok, gtok_hbm, in_sem.at[3])
    final.start()

    for cp in wswap:
        cp.wait_send()
    for cp in tell:
        cp.wait_send()
    for r in range(1, NZ):
        tell_home(r).wait_send()
    for c in range(nchunk):
        for g in range(NX):
            gone = send.at[chunks[c][0], pl.ds(g * GRP + MSG, GRP - MSG), lanes_of(c)]
            pltpu.make_async_copy(gone, gone, xs.at[c, g]).wait()
            if g > 0:
                along_y(c, g).wait_send()
    for n, (src, _, _, lane0, lanes) in enumerate(back_legs):
        for g in range(NX):
            gone = src.at[pl.ds(g * GRP + MSG, GRP - MSG), pl.ds(lane0, lanes)]
            pltpu.make_async_copy(gone, gone, bs.at[n, g]).wait()
            if g > 0:
                back_along_y(n, g).wait_send()
    gcopy.wait_send()
    dcopy.wait_send()
    for n in range(len(legs)):
        for s in range(1, 5):
            for k in range(2):
                hop(n, k, s).wait_send()
    for cp in outs:
        cp.wait()
    final.wait()


def finish(a0, a1, a2, a3, a4, o0, o1, o2, o3, o4, v0, v2, v3, v4, sem_in, sem_out):
    held = ((a0, v0, o0), (a2, v2, o2), (a3, v3, o3), (a4, v4, o4))
    ins = [pltpu.make_async_copy(a, v, sem_in.at[i]) for i, (a, v, _) in enumerate(held)]
    outs = [pltpu.make_async_copy(v, o, sem_out.at[i]) for i, (_, v, o) in enumerate(held)]
    for cp in ins:
        cp.start()
    o1[...] = a1[...].astype(BF)
    for cp, out in zip(ins, outs):
        cp.wait()
        out.start()
    for out in outs:
        out.wait()


def body(tokens, out_grad, expert_ids, gate_weights, keep_flags, gate_proj, up_proj, down_proj):
    width = tokens.shape[1]
    half = width // 2
    ff = gate_proj.shape[2]
    topn = expert_ids.shape[1]
    nexp = TOK
    wide = half + nexp
    any_spec = pl.BlockSpec(memory_space=pl.ANY)
    vmem = pl.BlockSpec(memory_space=pltpu.VMEM)
    dma = pltpu.SemaphoreType.DMA
    shapes = (
        jax.ShapeDtypeStruct(tokens.shape, BF),
        jax.ShapeDtypeStruct((topn, TOK), F32),
        jax.ShapeDtypeStruct(gate_proj.shape, BF),
        jax.ShapeDtypeStruct(up_proj.shape, BF),
        jax.ShapeDtypeStruct(down_proj.shape, BF),
    )
    scratch = [
        pltpu.VMEM((NZ * TOK, half), BF),
        pltpu.VMEM((NZ * TOK, half), BF),
        pltpu.VMEM((NZ * TOK, half), BF),
        pltpu.VMEM((NZ * TOK, half), BF),
        pltpu.VMEM((TOK, width), BF),
        pltpu.VMEM((NZ, 2 * topn, TOK), BF),
        pltpu.VMEM((NZ, PLANE, TOK), BF),
        pltpu.VMEM((NZ, PLANE, TOK), BF),
        pltpu.VMEM((PLANE, NZ * TOK), F32),
        pltpu.VMEM((PLANE, NZ * TOK), F32),
        pltpu.VMEM((SLOTS, NZ * TOK), BF),
        pltpu.VMEM((SLOTS, NZ * TOK), BF),
        pltpu.VMEM((4, SLOTS, half), BF),
        pltpu.VMEM((4, SLOTS - GRP, half), BF),
        pltpu.VMEM((4, SLOTS, half), BF),
        pltpu.VMEM((2, half, 2 * ff), BF),
        pltpu.VMEM((2, ff, half), BF),
        pltpu.VMEM((SLOTS, 2 * ff), F32),
        pltpu.VMEM((SLOTS, ff), F32),
        pltpu.VMEM((SLOTS, ff), BF),
        pltpu.VMEM((SLOTS, 2 * ff), BF),
        pltpu.VMEM((SLOTS, wide), BF),
        pltpu.VMEM((SLOTS, half), BF),
        pltpu.VMEM((SLOTS - GRP, wide), BF),
        pltpu.VMEM((SLOTS - GRP, half), BF),
        pltpu.VMEM((SLOTS, wide), BF),
        pltpu.VMEM((SLOTS, half), BF),
        pltpu.VMEM((8, TOK, half // 2), BF),
        pltpu.VMEM((8, TOK, half // 2), BF),
        pltpu.VMEM((8, TOK, half // 2), BF),
        pltpu.VMEM((8, TOK, half // 2), BF),
        pltpu.VMEM((8, TOK, half // 2), BF),
        pltpu.VMEM((8, TOK, half // 2), BF),
        pltpu.VMEM((8, TOK, half // 2), BF),
        pltpu.VMEM((8, TOK, half // 2), BF),
        pltpu.VMEM((half, 2 * ff), BF),
        pltpu.VMEM((ff, half), BF),
        pltpu.VMEM((half, 2 * ff), BF),
        pltpu.VMEM((ff, half), BF),
        pltpu.VMEM((half, 2 * ff), BF),
        pltpu.VMEM((ff, half), BF),
        pltpu.VMEM((TOK, width), BF),
        dma((4,)), dma((3,)), dma((3,)),
        dma((6, 2, 4)), dma((6, 2, 4)), dma((NZ,)), dma((NZ,)), dma((NZ,)), dma((NZ,)),
        dma((6, NX)), dma((6, NX)), dma((6, NX)), dma((6, NX)), dma((4, NX)), dma((4, NX)), dma((4, NX)), dma((4, NX)),
        dma((4, 8)), dma((4, 8)), dma((3,)), dma((3,)), dma((2,)), dma((2,)),
    ]
    done = pl.pallas_call(
        kernel,
        name="experts",
        out_shape=shapes,
        in_specs=[any_spec, any_spec, vmem, vmem, vmem, any_spec, any_spec, any_spec],
        out_specs=(any_spec, vmem, any_spec, any_spec, any_spec),
        scratch_shapes=scratch,
        compiler_params=pltpu.CompilerParams(
            collective_id=0, has_side_effects=True, vmem_limit_bytes=64 * 2**20 - 2**19
        ),
    )(tokens, out_grad, expert_ids.T, gate_weights.T, keep_flags.reshape(1, TOK), gate_proj, up_proj, down_proj)
    outs = pl.pallas_call(
        finish,
        name="finish",
        out_shape=(shapes[0], jax.ShapeDtypeStruct((topn, TOK), BF)) + shapes[2:],
        in_specs=[any_spec, vmem, any_spec, any_spec, any_spec],
        out_specs=(any_spec, vmem, any_spec, any_spec, any_spec),
        scratch_shapes=[pltpu.VMEM(shapes[i].shape, BF) for i in (0, 2, 3, 4)] + [dma((4,)), dma((4,))],
        compiler_params=pltpu.CompilerParams(vmem_limit_bytes=64 * 2**20 - 2**19),
    )(*done)
    return outs[0], outs[1].T, outs[2], outs[3], outs[4]


def solution(mesh):
    both = ("expert", "dp")
    in_specs = (
        P(both, None), P(both, None), P(both, None), P(both, None), P(both),
        P(both, None, None), P(both, None, None), P(both, None, None),
    )
    out_specs = (
        P(both, None), P(both, None), P(both, None, None), P(both, None, None), P(both, None, None),
    )
    return jax.shard_map(body, mesh=mesh, in_specs=in_specs, out_specs=out_specs, check_vma=False)
```

```python
import functools

import jax
import jax.numpy as jnp
from jax import lax
from jax.experimental import pallas as pl
from jax.experimental.pallas import tpu as pltpu
from jax.sharding import PartitionSpec as P

MESH = pl.DeviceIdType.MESH
BF = jnp.bfloat16
F32 = jnp.float32

TOK = 128
NZ = 8
NX = 4
CAP = 10
MSG = NZ * CAP
PLANE = NX * NX
SLOTS = PLANE * MSG
GRP = NX * MSG
FAR = (2, 1, 3, 0)
NN = (((1,), (0,)), ((), ()))
NT = (((1,), (1,)), ((), ()))
TN = (((0,), (0,)), ((), ()))


def mm(a, b, dims):
    return lax.dot_general(a, b, dims, preferred_element_type=F32)


def kernel(
    x_hbm, dy_hbm, ids_ref, gates_ref, keep_ref, wg_hbm, wu_hbm, wd_hbm,
    gtok_hbm, ggate_ref, ogg_hbm, ogu_hbm, ogd_hbm,
    ag0, ag1, ag2, ag3, dyraw, meta, told_out, told_in, pt, gt, oh, ohg, send, inter, recv, wgu, wd, gu, q, hid, dgu,
    ds0, ds1, rint0, rint1, ret0, ret1, rsa, rra, rsb, rrb, rsc, rrc, rsd, rrd, wsg, wsd, wrg, wrd, wog, wod, gtok,
    in_sem, w_sem, wout_sem,
    ags, agr, ms, mr, hs, hr, xs, xr, ys, yr, bs, br, cs, cr, rss, rsr, ws, wr, vs, vr,
):
    e = lax.axis_index("expert")
    d = lax.axis_index("dp")
    y, z = e // NZ, e % NZ
    x, core = d // 2, d % 2
    other = 1 - core

    def dev(dx, dy, dz):
        return (((y + dy + NX) % NX) * NZ + (z + dz + NZ) % NZ, ((x + dx + NX) % NX) * 2 + core)

    mate = (e, x * 2 + other)
    half = ag1.shape[1]
    hidn = hid.shape[1]
    nexp = TOK
    ags_bufs = [ag0, ag1, ag2, ag3]
    quarter = half // 2
    chunks = [(0, 0, quarter), (0, quarter, quarter), (1, 0, half), (2, 0, half), (3, 0, quarter), (3, quarter, quarter)]
    starts = [0, 0, 1, 3, 5, 6]
    nchunk = len(chunks)

    incp = [
        pltpu.make_async_copy(x_hbm.at[:, 0:half], ag0.at[0:TOK], in_sem.at[0]),
        pltpu.make_async_copy(x_hbm.at[:, half:2 * half], ag1.at[0:TOK], in_sem.at[1]),
        pltpu.make_async_copy(dy_hbm, dyraw, in_sem.at[2]),
    ]
    for cp in incp:
        cp.start()
    wl = [
        pltpu.make_async_copy(wg_hbm.at[0], wgu.at[core, :, 0:hidn], w_sem.at[0]),
        pltpu.make_async_copy(wu_hbm.at[0], wgu.at[core, :, hidn:2 * hidn], w_sem.at[1]),
        pltpu.make_async_copy(wd_hbm.at[0], wd.at[core], w_sem.at[2]),
    ]

    bar = pltpu.get_barrier_semaphore()
    for dz in range(1, NZ):
        pl.semaphore_signal(bar, inc=1, device_id=dev(0, 0, dz), device_id_type=MESH)
    pl.semaphore_signal(bar, inc=1, device_id=mate, device_id_type=MESH)
    for k in range(1, NX):
        pl.semaphore_signal(bar, inc=1, device_id=dev(k, 0, 0), device_id_type=MESH)
        pl.semaphore_signal(bar, inc=1, device_id=dev(0, k, 0), device_id_type=MESH)

    topn = ids_ref.shape[0]
    meta[0] = jnp.concatenate([ids_ref[...].astype(F32), gates_ref[...].astype(F32)], axis=0).astype(BF)
    pl.semaphore_wait(bar, 2 * (NX - 1) + NZ)

    def remote(src, dst, s, r, to):
        return pltpu.make_async_remote_copy(
            src_ref=src, dst_ref=dst, send_sem=s, recv_sem=r, device_id=to, device_id_type=MESH
        )

    def block(k):
        return pl.ds(k * TOK, TOK)

    def gather_copies(c, s):
        buf, lane0, lanes = chunks[c]
        ag = ags_bufs[buf]
        a, b = (9 - s) % NZ, 8 - s
        lo = hi = pl.ds(lane0, lanes)
        if s == 4:
            if lanes > nexp:
                lo, hi = pl.ds(lane0, lanes // 2), pl.ds(lane0 + lanes // 2, lanes // 2)
        ways = [
            (ag.at[block(s - 1), lo], ag.at[block(s), lo], ags.at[c, 0, s - 1], agr.at[c, 0, s - 1], dev(0, 0, 1)),
            (ag.at[block(a), hi], ag.at[block(b), hi], ags.at[c, 1, s - 1], agr.at[c, 1, s - 1], dev(0, 0, -1)),
        ]
        return [remote(*way) for way in (ways[c:c + 1] if s == 4 and lanes == nexp else ways)]

    def ag_start(c):
        for cp in gather_copies(c, 1):
            cp.start()

    def ag_step(c, s):
        for cp in gather_copies(c, s):
            cp.wait_recv()
        if s < 4:
            for cp in gather_copies(c, s + 1):
                cp.start()

    tell = [remote(meta.at[0], meta.at[k], ms.at[k], mr.at[k], dev(0, 0, k)) for k in range(1, NZ)]
    for cp in tell:
        cp.start()
    incp[0].wait()
    for c in range(nchunk):
        if starts[c] == 0:
            ag_start(c)
    wswap = [
        remote(wg_hbm.at[0], wgu.at[core, :, 0:hidn], ws.at[0], wr.at[0], mate),
        remote(wu_hbm.at[0], wgu.at[core, :, hidn:2 * hidn], ws.at[1], wr.at[1], mate),
        remote(wd_hbm.at[0], wd.at[core], ws.at[2], wr.at[2], mate),
    ]
    wrecv = [
        remote(wg_hbm.at[0], wgu.at[other, :, 0:hidn], ws.at[0], wr.at[0], mate),
        remote(wu_hbm.at[0], wgu.at[other, :, hidn:2 * hidn], ws.at[1], wr.at[1], mate),
        remote(wd_hbm.at[0], wd.at[other], ws.at[2], wr.at[2], mate),
    ]

    row = lax.broadcasted_iota(jnp.int32, (TOK, TOK), 0)
    col = lax.broadcasted_iota(jnp.int32, (TOK, TOK), 1)
    row16 = lax.broadcasted_iota(jnp.int32, (PLANE, TOK), 0)
    wanted = (((y + row16 // NX) % NX) * (NZ * NX) + z * NX + (x + row16 % NX) % NX).astype(F32)
    earlier = jnp.where(row < col, 1.0, 0.0).astype(BF)
    col16 = lax.broadcasted_iota(jnp.int32, (PLANE, TOK), 1).astype(F32)
    pick = jnp.where(col16 == wanted, 1.0, 0.0).astype(BF)

    def route(r):
        told = meta[r].astype(F32)
        mine = jnp.zeros((PLANE, TOK), F32)
        weight = mine
        for j in range(topn):
            hit = wanted == told[j:j + 1, :]
            mine = jnp.where(hit, 1.0, mine)
            weight = jnp.where(hit, told[topn + j:topn + j + 1, :], weight)
        gt[:, r * TOK:(r + 1) * TOK] = weight
        place = mm(mine.astype(BF), earlier, NN)
        pt[:, r * TOK:(r + 1) * TOK] = jnp.where(mine > 0.5, place, -1.0)

    def mask_rows():
        incp[2].wait()
        keep = jnp.where(row == col, keep_ref[...].astype(F32), 0.0).astype(BF)
        ag2[0:TOK, :] = mm(keep, dyraw[:, 0:half], NN).astype(BF)
        ag3[0:TOK, :] = mm(keep, dyraw[:, half:2 * half], NN).astype(BF)

    prow = lax.broadcasted_iota(jnp.int32, (MSG, NZ * TOK), 0)
    pcol = lax.broadcasted_iota(jnp.int32, (MSG, NZ * TOK), 1)
    pattern = jnp.where(prow // CAP == pcol // TOK, prow % CAP, -2).astype(F32)

    def build(j, carry):
        rows = pl.ds(pl.multiple_of(j * MSG, MSG), MSG)
        oh[rows, :] = jnp.where(pattern == pt[pl.ds(j, 1), :], 1.0, 0.0).astype(BF)
        return carry

    def build_gated(j, carry):
        rows = pl.ds(pl.multiple_of(j * MSG, MSG), MSG)
        ohg[rows, :] = jnp.where(pattern == pt[pl.ds(j, 1), :], gt[pl.ds(j, 1), :], 0.0).astype(BF)
        return carry

    def rows_of(g):
        return pl.ds(pl.multiple_of(g * GRP, GRP), GRP)

    def lanes_of(c):
        return pl.ds(chunks[c][1], chunks[c][2])

    def hand_out(c, g):
        buf, at, width = chunks[c]
        sel = oh if buf < 2 else ohg
        res = mm(sel[g * GRP:(g + 1) * GRP, :], ags_bufs[buf][:, at:at + width], NN).astype(BF)
        target, base = (recv, 0) if g == 0 else (inter, (g - 1) * GRP)
        target[buf, base:base + MSG, at:at + width] = res[0:MSG]
        send[buf, g * GRP + MSG:(g + 1) * GRP, at:at + width] = res[MSG:]
        for dx in FAR[:3]:
            remote(send.at[buf, pl.ds(g * GRP + dx * MSG, MSG), lanes_of(c)],
                   target.at[buf, pl.ds(base + dx * MSG, MSG), lanes_of(c)],
                   xs.at[c, g], xr.at[c, g], dev(dx, 0, 0)).start()

    def along_y(c, g):
        buf = chunks[c][0]
        return remote(inter.at[buf, pl.ds((g - 1) * GRP, GRP), lanes_of(c)], recv.at[buf, pl.ds(g * GRP, GRP), lanes_of(c)],
                      ys.at[c, g], yr.at[c, g], dev(0, g, 0))

    def pass_on(c, g):
        came = inter.at[chunks[c][0], pl.ds((g - 1) * GRP + MSG, GRP - MSG), lanes_of(c)]
        pltpu.make_async_copy(came, came, xr.at[c, g]).wait()
        along_y(c, g).start()

    def landed(c, g):
        if g == 0:
            came = recv.at[chunks[c][0], pl.ds(MSG, GRP - MSG), lanes_of(c)]
            pltpu.make_async_copy(came, came, xr.at[c, 0]).wait()
        else:
            along_y(c, g).wait_recv()

    def tick(t, first=0, end=nchunk):
        for c in range(first, end):
            if 1 <= t - starts[c] <= 4:
                ag_step(c, t - starts[c])
        for c in range(first, end):
            if t == starts[c]:
                if c == 3:
                    mask_rows()
                ag_start(c)

    ag_step(0, 1)
    route(0)
    ag_step(1, 1)
    incp[1].wait()
    ag_start(2)
    ag_step(0, 2)
    for cp in tell:
        cp.wait_recv()
    for r in range(1, NZ):
        route(r)
    ag_step(1, 2)
    ag_step(0, 3)
    lax.fori_loop(0, PLANE, build, 0)
    ag_step(2, 1)
    ag_step(1, 3)
    ag_step(0, 4)

    def first_layer(h):
        for c in range(nchunk):
            if chunks[c][0] == h:
                for g in range(NX):
                    landed(c, g)

        def first(g, carry):
            part = mm(recv[h, rows_of(g), :], wgu[h], NN)
            if h == 0:
                gu[rows_of(g), :] = part
            else:
                gu[rows_of(g), :] = gu[rows_of(g), :] + part
            return carry

        lax.fori_loop(0, NX, first, 0)

    SUB = 32

    def activation(i, carry):
        rows = pl.ds(pl.multiple_of(i * SUB, SUB), SUB)
        gpre = gu[rows, 0:hidn]
        upre = gu[rows, hidn:2 * hidn]
        sig = jax.nn.sigmoid(gpre)
        swish = gpre * sig
        hid[rows, :] = (swish * upre).astype(BF)
        gu[rows, 0:hidn] = upre * sig * (1.0 + gpre * (1.0 - sig))
        gu[rows, hidn:2 * hidn] = swish
        return carry

    for c in range(nchunk):
        if c == 1:
            for cp in wl:
                cp.start()
            for cp in wswap:
                cp.start()
        if chunks[c][0] == 2:
            lax.fori_loop(0, PLANE, build_gated, 0)
        ahead = list(range(starts[c] + 5, starts[c + 1] + 5)) if c + 1 < nchunk else []
        for i, g in enumerate(FAR):
            hand_out(c, g)
            if c == 0 and i == 0:
                tick(3, 2)
            if c == 0 and i == 2:
                ag_step(1, 4)
                tick(4, 2)
            if c == nchunk - 2 and i == 0:
                for cp in wl:
                    cp.wait()
                for cp in wrecv:
                    cp.wait_recv()
                first_layer(0)
            if c == nchunk - 1 and i == 0:
                first_layer(1)
            if c == nchunk - 1 and i == 1:
                lax.fori_loop(0, SLOTS // SUB, activation, 0)
            if c > 0 and g > 0:
                pass_on(c - 1, g)
            if i < len(ahead) - 1:
                tick(ahead[i])
        for t in ahead[3:] if len(ahead) > 4 else ahead[-1:]:
            tick(t)

    for g in FAR[:3]:
        pass_on(nchunk - 1, g)

    for c in range(nchunk):
        for s in range(1, 5):
            for cp in gather_copies(c, s):
                cp.wait_send()

    def turn(m, carry):
        cols = pl.ds(pl.multiple_of(m * TOK, TOK), TOK)
        turned = jnp.transpose(oh[:, cols])
        ag0[cols, :] = turned[:, 0:half]
        ag1[cols, :] = turned[:, half:2 * half]
        ag2[cols, 0:SLOTS - 2 * half] = turned[:, 2 * half:SLOTS]
        return carry

    lax.fori_loop(0, NZ, turn, 0)

    for g in range(NX):
        landed(3, g)

    def back(g, carry):
        q[rows_of(g), :] = mm(recv[2, rows_of(g), :], wd[0], NT)
        return carry

    lax.fori_loop(0, NX, back, 0)

    expert_lane = y * (NZ * NX) + z * NX + x
    lane = lax.broadcasted_iota(jnp.int32, (SUB, TOK), 1)
    wide = half + nexp
    back_legs = [
        (ds0, rint0, ret0, 0, nexp + quarter),
        (ds0, rint0, ret0, nexp + quarter, quarter),
        (ds1, rint1, ret1, 0, quarter),
        (ds1, rint1, ret1, quarter, quarter),
    ]

    def send_back(n, g):
        src, mid, end, lane0, lanes = back_legs[n]
        target, base = (end, 0) if g == 0 else (mid, (g - 1) * GRP)
        for dx in FAR[:3]:
            remote(src.at[pl.ds(g * GRP + dx * MSG, MSG), pl.ds(lane0, lanes)],
                   target.at[pl.ds(base + dx * MSG, MSG), pl.ds(lane0, lanes)],
                   bs.at[n, g], br.at[n, g], dev(-dx, 0, 0)).start()

    def back_along_y(n, g):
        _, mid, end, lane0, lanes = back_legs[n]
        return remote(mid.at[pl.ds((g - 1) * GRP, GRP), pl.ds(lane0, lanes)],
                      end.at[pl.ds(g * GRP, GRP), pl.ds(lane0, lanes)], cs.at[n, g], cr.at[n, g], dev(0, -g, 0))

    def pass_back(n, g):
        _, mid, _, lane0, lanes = back_legs[n]
        came = mid.at[pl.ds((g - 1) * GRP + MSG, GRP - MSG), pl.ds(lane0, lanes)]
        pltpu.make_async_copy(came, came, br.at[n, g]).wait()
        back_along_y(n, g).start()

    def returned(n, g):
        _, _, end, lane0, lanes = back_legs[n]
        if g == 0:
            came = end.at[pl.ds(MSG, GRP - MSG), pl.ds(lane0, lanes)]
            pltpu.make_async_copy(came, came, br.at[n, 0]).wait()
        else:
            back_along_y(n, g).wait_recv()

    def keep_or_send(src, mid, end, g, lanes, value):
        target, base = (end, 0) if g == 0 else (mid, (g - 1) * GRP)
        target[base:base + MSG, lanes] = value[0:MSG]
        src[g * GRP + MSG:(g + 1) * GRP, lanes] = value[MSG:]

    def second(g):
        landed(4, g)
        landed(5, g)
        group = slice(g * GRP, (g + 1) * GRP)
        q[group, :] = q[group, :] + mm(recv[3, group, :], wd[1], NT)

        def grads(k, inner):
            rows = pl.ds(pl.multiple_of(g * GRP + k * SUB, SUB), SUB)
            dh = q[rows, :]
            dgu[rows, 0:hidn] = (dh * gu[rows, 0:hidn]).astype(BF)
            dgu[rows, hidn:2 * hidn] = (dh * gu[rows, hidn:2 * hidn]).astype(BF)
            dot = jnp.sum(dh * hid[rows, :].astype(F32), axis=1, keepdims=True)
            ds0[rows, 0:nexp] = jnp.where(lane == expert_lane, dot, 0.0).astype(BF)
            return inner

        lax.fori_loop(0, GRP // SUB, grads, 0)
        keep_or_send(ds0, rint0, ret0, g, slice(nexp, wide), mm(dgu[group, :], wgu[0], NT).astype(BF))
        target, base = (ret0, 0) if g == 0 else (rint0, (g - 1) * GRP)
        target[base:base + MSG, 0:nexp] = ds0[g * GRP:g * GRP + MSG, 0:nexp]
        if g > 0:
            send_back(0, g)

    def third(g):
        group = slice(g * GRP, (g + 1) * GRP)
        keep_or_send(ds1, rint1, ret1, g, slice(0, half), mm(dgu[group, :], wgu[1], NT).astype(BF))
        send_back(2, g)

    for g in (0, 2, 1, 3):
        second(g)
    send_back(0, 0)
    for g in FAR:
        send_back(1, g)
    third(2)
    third(1)
    pass_back(0, 2)
    third(3)
    pass_back(0, 1)
    third(0)
    pass_back(0, 3)
    for g in FAR:
        send_back(3, g)

    MT = 256

    def other_gu(m, carry):
        cols = pl.ds(pl.multiple_of(m * MT, MT), MT)
        wsg[cols, :] = mm(recv[other, :, cols], dgu[...], TN).astype(BF)
        return carry

    lax.fori_loop(0, half // MT, other_gu, 0)
    gcopy = remote(wsg, wrg, vs.at[0], vr.at[0], mate)
    gcopy.start()
    pass_back(1, 2)
    pass_back(1, 1)
    wsd[...] = mm(hid[...], recv[2 + other], TN).astype(BF)
    dcopy = remote(wsd, wrd, vs.at[1], vr.at[1], mate)
    dcopy.start()

    outs = [
        pltpu.make_async_copy(wog.at[:, 0:hidn], ogg_hbm.at[0], wout_sem.at[0]),
        pltpu.make_async_copy(wog.at[:, hidn:2 * hidn], ogu_hbm.at[0], wout_sem.at[1]),
        pltpu.make_async_copy(wod, ogd_hbm.at[0], wout_sem.at[2]),
    ]

    def own_gu(m, carry):
        cols = pl.ds(pl.multiple_of(m * MT, MT), MT)
        wog[cols, :] = (mm(recv[core, :, cols], dgu[...], TN) + wrg[cols, :].astype(F32)).astype(BF)
        return carry

    def own_grads():
        gcopy.wait_recv()
        lax.fori_loop(0, half // MT, own_gu, 0)
        outs[0].start()
        outs[1].start()
        dcopy.wait_recv()
        wod[...] = (mm(hid[...], recv[2 + core], TN) + wrd[...].astype(F32)).astype(BF)
        outs[2].start()

    legs = [
        (ret0, nexp, quarter, nexp, rsa, rra, 0),
        (ret0, nexp + quarter, quarter, nexp, rsb, rrb, quarter),
        (ret1, 0, quarter, nexp, rsc, rrc, half),
        (ret1, quarter, quarter, nexp, rsd, rrd, half + quarter),
    ]

    def part(n, r):
        width, at = legs[n][2], legs[n][6]
        return gu[r * TOK:(r + 1) * TOK, at:at + width]

    def hop(n, k, s):
        _, _, width, cut, sbuf, rbuf, _ = legs[n]
        lanes = pl.ds(0, width)
        if s == 1:
            lanes = pl.ds(0, cut) if k == 0 else pl.ds(cut, width - cut)
        slot = k * 4 + s - 1
        return remote(sbuf.at[slot, :, lanes], rbuf.at[slot, :, lanes], rss.at[n, slot], rsr.at[n, slot],
                      dev(0, 0, -1 if k == 0 else 1))

    def begin(n, k, s):
        _, _, width, cut, sbuf, rbuf, _ = legs[n]
        slot = k * 4 + s - 1
        full = part(n, 4 if s == 1 else (5 - s if k == 0 else 3 + s))
        if s == 1:
            if k == 0:
                sbuf[slot, :, 0:cut] = full[:, 0:cut].astype(BF)
            else:
                sbuf[slot, :, cut:width] = full[:, cut:width].astype(BF)
        elif s == 2 and k == 0:
            sbuf[slot, :, 0:cut] = (full[:, 0:cut] + rbuf[slot - 1, :, 0:cut].astype(F32)).astype(BF)
            sbuf[slot, :, cut:width] = full[:, cut:width].astype(BF)
        elif s == 2:
            sbuf[slot, :, 0:cut] = full[:, 0:cut].astype(BF)
            sbuf[slot, :, cut:width] = (full[:, cut:width] + rbuf[slot - 1, :, cut:width].astype(F32)).astype(BF)
        else:
            sbuf[slot, :, :] = (full + rbuf[slot - 1].astype(F32)).astype(BF)
        hop(n, k, s).start()

    def step(n, s):
        for k in range(2):
            hop(n, k, s - 1).wait_recv()
            begin(n, k, s)

    def select(cols, ret, came):
        return (
            mm(ag0[cols, :], ret[0:half, came], NN)
            + mm(ag1[cols, :], ret[half:2 * half, came], NN)
            + mm(ag2[cols, 0:SLOTS - 2 * half], ret[2 * half:SLOTS, came], NN)
        )

    def tell_home(r):
        return remote(told_out.at[r], told_in.at[r], hs.at[r], hr.at[r], dev(0, 0, -r))

    def gates_home():
        def turn_back(m, carry):
            cols = pl.ds(pl.multiple_of(m * MT, MT), MT)
            found = mm(pick, select(cols, ret0, slice(0, nexp)).astype(BF), NT).astype(BF)
            for r in range(MT // TOK):
                told_out[m * (MT // TOK) + r] = found[:, r * TOK:(r + 1) * TOK]
            return carry

        lax.fori_loop(0, NZ * TOK // MT, turn_back, 0)
        for r in range(1, NZ):
            tell_home(r).start()

    def leave(n):
        ret, lane0, width, _, _, _, at = legs[n]
        for g in range(NX):
            returned(n, g)

        def combine(i, carry):
            cols = pl.ds(pl.multiple_of(lax.rem(i + 2, 4) * MT, MT), MT)
            gu[cols, at:at + width] = select(cols, ret, slice(lane0, lane0 + width))
            return carry

        lax.fori_loop(0, 1, combine, 0)
        for k in range(2):
            begin(n, k, 1)
        lax.fori_loop(1, NZ * TOK // MT, combine, 0)

    def total(n):
        for k in range(2):
            hop(n, k, 4).wait_recv()
        rbuf = legs[n][5]
        return part(n, 0) + rbuf[3].astype(F32) + rbuf[7].astype(F32)

    pass_back(1, 3)

    leave(0)

    @pl.when(core == 0)
    def _():
        own_grads()

    for g in FAR[:3]:
        pass_back(2, g)
    step(0, 2)
    gates_home()
    for g in FAR[:3]:
        pass_back(3, g)
    leave(1)
    step(0, 3)
    step(1, 2)
    leave(2)
    step(0, 4)
    step(1, 3)
    step(2, 2)
    leave(3)
    step(1, 4)
    step(2, 3)
    step(3, 2)
    gtok[:, 0:quarter] = total(0).astype(BF)
    for r in range(1, NZ):
        tell_home(r).wait_recv()
    there = [told_out[0].astype(F32)] + [told_in[r].astype(F32) for r in range(1, NZ)]
    names = [((y + row16 // NX) % NX) * (NZ * NX) + ((z + r) % NZ) * NX + (x + row16 % NX) % NX for r in range(NZ)]
    for j in range(topn):
        value = jnp.zeros((PLANE, TOK), F32)
        for r in range(NZ):
            value = jnp.where(names[r] == ids_ref[j:j + 1, :], there[r], value)
        value = jnp.sum(value, axis=0, keepdims=True)
        ggate_ref[j:j + 1, :] = value / gates_ref[j:j + 1, :].astype(F32)

    @pl.when(core == 1)
    def _():
        own_grads()

    step(2, 4)
    step(3, 3)
    gtok[:, quarter:half] = total(1).astype(BF)
    step(3, 4)
    gtok[:, half:half + quarter] = total(2).astype(BF)
    gtok[:, half + quarter:2 * half] = total(3).astype(BF)
    final = pltpu.make_async_copy(gtok, gtok_hbm, in_sem.at[3])
    final.start()

    for cp in wswap:
        cp.wait_send()
    for cp in tell:
        cp.wait_send()
    for r in range(1, NZ):
        tell_home(r).wait_send()
    for c in range(nchunk):
        for g in range(NX):
            gone = send.at[chunks[c][0], pl.ds(g * GRP + MSG, GRP - MSG), lanes_of(c)]
            pltpu.make_async_copy(gone, gone, xs.at[c, g]).wait()
            if g > 0:
                along_y(c, g).wait_send()
    for n, (src, _, _, lane0, lanes) in enumerate(back_legs):
        for g in range(NX):
            gone = src.at[pl.ds(g * GRP + MSG, GRP - MSG), pl.ds(lane0, lanes)]
            pltpu.make_async_copy(gone, gone, bs.at[n, g]).wait()
            if g > 0:
                back_along_y(n, g).wait_send()
    gcopy.wait_send()
    dcopy.wait_send()
    for n in range(len(legs)):
        for s in range(1, 5):
            for k in range(2):
                hop(n, k, s).wait_send()
    for cp in outs:
        cp.wait()
    final.wait()


def finish(a0, a1, a2, a3, a4, o0, o1, o2, o3, o4, v0, v2, v3, v4, sem_in, sem_out):
    held = []
    for a, v, o in ((a2, v2, o2), (a3, v3, o3), (a4, v4, o4), (a0, v0, o0)):
        if len(a.shape) == 3:
            a, v, o = a.at[0], v.at[0], o.at[0]
        rows = a.shape[0] // 2
        held += [tuple(ref.at[pl.ds(k * rows, rows)] for ref in (a, v, o)) for k in range(2)]
    ins = [pltpu.make_async_copy(a, v, sem_in.at[i]) for i, (a, v, _) in enumerate(held)]
    outs = [pltpu.make_async_copy(v, o, sem_out.at[i]) for i, (_, v, o) in enumerate(held)]
    for cp in ins:
        cp.start()
    o1[...] = a1[...].astype(BF)
    for cp, out in zip(ins, outs):
        cp.wait()
        out.start()
    for out in outs:
        out.wait()


def body(tokens, out_grad, expert_ids, gate_weights, keep_flags, gate_proj, up_proj, down_proj):
    width = tokens.shape[1]
    half = width // 2
    ff = gate_proj.shape[2]
    topn = expert_ids.shape[1]
    nexp = TOK
    wide = half + nexp
    any_spec = pl.BlockSpec(memory_space=pl.ANY)
    vmem = pl.BlockSpec(memory_space=pltpu.VMEM)
    dma = pltpu.SemaphoreType.DMA
    shapes = (
        jax.ShapeDtypeStruct(tokens.shape, BF),
        jax.ShapeDtypeStruct((topn, TOK), F32),
        jax.ShapeDtypeStruct(gate_proj.shape, BF),
        jax.ShapeDtypeStruct(up_proj.shape, BF),
        jax.ShapeDtypeStruct(down_proj.shape, BF),
    )
    scratch = [
        pltpu.VMEM((NZ * TOK, half), BF),
        pltpu.VMEM((NZ * TOK, half), BF),
        pltpu.VMEM((NZ * TOK, half), BF),
        pltpu.VMEM((NZ * TOK, half), BF),
        pltpu.VMEM((TOK, width), BF),
        pltpu.VMEM((NZ, 2 * topn, TOK), BF),
        pltpu.VMEM((NZ, PLANE, TOK), BF),
        pltpu.VMEM((NZ, PLANE, TOK), BF),
        pltpu.VMEM((PLANE, NZ * TOK), F32),
        pltpu.VMEM((PLANE, NZ * TOK), F32),
        pltpu.VMEM((SLOTS, NZ * TOK), BF),
        pltpu.VMEM((SLOTS, NZ * TOK), BF),
        pltpu.VMEM((4, SLOTS, half), BF),
        pltpu.VMEM((4, SLOTS - GRP, half), BF),
        pltpu.VMEM((4, SLOTS, half), BF),
        pltpu.VMEM((2, half, 2 * ff), BF),
        pltpu.VMEM((2, ff, half), BF),
        pltpu.VMEM((SLOTS, 2 * ff), F32),
        pltpu.VMEM((SLOTS, ff), F32),
        pltpu.VMEM((SLOTS, ff), BF),
        pltpu.VMEM((SLOTS, 2 * ff), BF),
        pltpu.VMEM((SLOTS, wide), BF),
        pltpu.VMEM((SLOTS, half), BF),
        pltpu.VMEM((SLOTS - GRP, wide), BF),
        pltpu.VMEM((SLOTS - GRP, half), BF),
        pltpu.VMEM((SLOTS, wide), BF),
        pltpu.VMEM((SLOTS, half), BF),
        pltpu.VMEM((8, TOK, half // 2), BF),
        pltpu.VMEM((8, TOK, half // 2), BF),
        pltpu.VMEM((8, TOK, half // 2), BF),
        pltpu.VMEM((8, TOK, half // 2), BF),
        pltpu.VMEM((8, TOK, half // 2), BF),
        pltpu.VMEM((8, TOK, half // 2), BF),
        pltpu.VMEM((8, TOK, half // 2), BF),
        pltpu.VMEM((8, TOK, half // 2), BF),
        pltpu.VMEM((half, 2 * ff), BF),
        pltpu.VMEM((ff, half), BF),
        pltpu.VMEM((half, 2 * ff), BF),
        pltpu.VMEM((ff, half), BF),
        pltpu.VMEM((half, 2 * ff), BF),
        pltpu.VMEM((ff, half), BF),
        pltpu.VMEM((TOK, width), BF),
        dma((4,)), dma((3,)), dma((3,)),
        dma((6, 2, 4)), dma((6, 2, 4)), dma((NZ,)), dma((NZ,)), dma((NZ,)), dma((NZ,)),
        dma((6, NX)), dma((6, NX)), dma((6, NX)), dma((6, NX)), dma((4, NX)), dma((4, NX)), dma((4, NX)), dma((4, NX)),
        dma((4, 8)), dma((4, 8)), dma((3,)), dma((3,)), dma((2,)), dma((2,)),
    ]
    done = pl.pallas_call(
        kernel,
        name="experts",
        out_shape=shapes,
        in_specs=[any_spec, any_spec, vmem, vmem, vmem, any_spec, any_spec, any_spec],
        out_specs=(any_spec, vmem, any_spec, any_spec, any_spec),
        scratch_shapes=scratch,
        compiler_params=pltpu.CompilerParams(
            collective_id=0, has_side_effects=True, vmem_limit_bytes=64 * 2**20 - 2**19
        ),
    )(tokens, out_grad, expert_ids.T, gate_weights.T, keep_flags.reshape(1, TOK), gate_proj, up_proj, down_proj)
    outs = pl.pallas_call(
        finish,
        name="finish",
        out_shape=(shapes[0], jax.ShapeDtypeStruct((topn, TOK), BF)) + shapes[2:],
        in_specs=[any_spec, vmem, any_spec, any_spec, any_spec],
        out_specs=(any_spec, vmem, any_spec, any_spec, any_spec),
        scratch_shapes=[pltpu.VMEM(shapes[i].shape, BF) for i in (0, 2, 3, 4)] + [dma((8,)), dma((8,))],
        compiler_params=pltpu.CompilerParams(vmem_limit_bytes=64 * 2**20 - 2**19),
    )(*done)
    return outs[0], outs[1].T, outs[2], outs[3], outs[4]


def solution(mesh):
    both = ("expert", "dp")
    in_specs = (
        P(both, None), P(both, None), P(both, None), P(both, None), P(both),
        P(both, None, None), P(both, None, None), P(both, None, None),
    )
    out_specs = (
        P(both, None), P(both, None), P(both, None, None), P(both, None, None), P(both, None, None),
    )
    return jax.shard_map(body, mesh=mesh, in_specs=in_specs, out_specs=out_specs, check_vma=False)
```
